32 devices in a mesh: groups: 2 (over y), gx: 4 (over z), gy: 2 (over x), gz: 2 (over core).
Axes of the slice: x: 2, y: 2, z: 4, core: 2. Of those that a mesh axis runs over, the one named last changes fastest.
Arguments:
- positions: float32 [3, 8, 2, 2, 128], P(None, ('groups', 'gx'), 'gy', 'gz'), parts along dimension 1, may hold values from 0 to 1
- species: int32 [8, 2, 2, 128], P(('groups', 'gx'), 'gy', 'gz'), parts along dimension 0, may hold values from 0 to 4
- neighbours: int32 [8, 2, 2, 16, 128], P(('groups', 'gx'), 'gy', 'gz'), parts along dimension 0, may hold values from -1 to 559, as said below
- send_list: int32 [8, 2, 2, 16], P(('groups', 'gx'), 'gy', 'gz'), parts along dimension 0, may hold values from 0 to 127, as said below
- embedding: float32 [5, 128], replicated, may hold values from -6 to 6
- radial_in: float32 [8, 64], replicated, may hold values from -3 to 3
- radial_out_one: float32 [64, 256], replicated, may hold values from -0.1875 to 0.1875
- radial_in_two: float32 [8, 64], replicated, may hold values from -3 to 3
- radial_out_two: float32 [64, 512], replicated, may hold values from -0.1875 to 0.1875
- mix_scalar_one: float32 [128, 128], replicated, may hold values from -0.5 to 0.5
- mix_square_one: float32 [128, 128], replicated, may hold values from -0.25 to 0.25
- mix_vector_one: float32 [128, 128], replicated, may hold values from -0.5 to 0.5
- mix_scalar_two: float32 [128, 128], replicated, may hold values from -0.5 to 0.5
- mix_square_two: float32 [128, 128], replicated, may hold values from -0.1875 to 0.1875
- readout: float32 [128], replicated, may hold values from -1 to 1
Outputs:
- forces: float32 [3, 8, 2, 2, 128], P(None, ('groups', 'gx'), 'gy', 'gz'), parts along dimension 1
- atom_energy: float32 [8, 2, 2, 128], P(('groups', 'gx'), 'gy', 'gz'), parts along dimension 0
The draws below stay inside these ranges and needn't reach their ends.
There are 2 independent parts, one for each index of `groups`. The reference program is written for one: setup_inputs(seed, part) draws one part's arguments, and reference() takes and returns one part's arrays. A program takes and returns all parts, laid end to end along the dimension named above; an argument that names none is the same for every part. Nothing has to cross between parts.
Inputs may be any that keep to these rules, and one draw needn't show every extreme that they name: `neighbours`: each entry is -1 (an empty slot) or an index into the extended list of 560 atoms; it never names the atom itself nor block 13; empty slots of an atom come after its used ones; an atom has at least 8 used slots, and in every domain some atom uses all 16. `send_list`: 16 distinct atoms of the domain.
All inputs are finite; a program needn't handle non-finite values.
Results may differ from the reference program's by a relative error of at most 0.0003.
Values sent between devices are 32-bit elements; how exact they have to be, the bound alone decides.
No kernel may reach another device: no remote copies, remote signals or barrier semaphores. Data moves between devices by JAX's collectives and lax.ppermute only.
A program may use at most 128 MiB of HBM per device.

```python
import jax
import jax.numpy as jnp
from jax import lax

C = 128
RH = 64
RB = 8
SPECIES = 5
NB = 16
A_DEV = 128
G_DEV = 16
DX = 4
DY = 2
DZ = 2


def pick_ghosts(domain_key):
    return jax.random.permutation(domain_key, A_DEV)[:G_DEV]


def draw_send_list(key, part):
    key = jax.random.fold_in(key, 7)
    domain_keys = jax.random.split(key, DX * DY * DZ)
    picks = jax.vmap(pick_ghosts)(domain_keys)
    return picks.reshape(DX, DY, DZ, G_DEV).astype(jnp.int32)


def draw_neighbours(key, part):
    key = jax.random.fold_in(key, 11)
    pick_key, count_key = jax.random.split(key)
    shape = (DX, DY, DZ, NB, A_DEV)
    candidates = jax.random.randint(pick_key, shape, 0, A_DEV - 1 + 26 * G_DEV).astype(jnp.int32)
    atom_ids = jnp.arange(A_DEV, dtype=jnp.int32)
    own_index = candidates + (candidates >= atom_ids).astype(jnp.int32)
    ghost_rank = candidates - (A_DEV - 1)
    ghost_slot = ghost_rank // G_DEV
    ghost_slot = ghost_slot + (ghost_slot >= 13).astype(jnp.int32)
    ghost_index = A_DEV + ghost_slot * G_DEV + ghost_rank % G_DEV
    chosen = jnp.where(candidates < A_DEV - 1, own_index, ghost_index)
    counts = jax.random.randint(count_key, (DX, DY, DZ, 1, A_DEV), NB // 2, NB + 1).astype(jnp.int32)
    counts = counts.at[..., 0].set(NB)
    slot_ids = jnp.arange(NB, dtype=jnp.int32)[:, None]
    return jnp.where(slot_ids < counts, chosen, -1).astype(jnp.int32)


def signed_magnitudes(key, lowest, highest):
    sign_key, size_key = jax.random.split(key)
    signs = jnp.where(jax.random.bernoulli(sign_key, 0.5, (RB, RH)), 1.0, -1.0).astype(jnp.float32)
    sizes = jax.random.uniform(size_key, (RB, RH), jnp.float32, lowest, highest)
    return (signs * sizes).astype(jnp.float32)


def draw_radial_in(key, part):
    key = jax.random.fold_in(key, 23)
    return signed_magnitudes(key, 2.0, 3.0)


def draw_radial_in_two(key, part):
    key = jax.random.fold_in(key, 29)
    return signed_magnitudes(key, 2.0, 3.0)


def touch_ends(result, rng, low, high):
    longest = result.shape.index(max(result.shape))
    spots = []
    for shift in (0, 1):
        where = [jax.random.randint(jax.random.fold_in(rng, axis), (), 0, length) for axis, length in enumerate(result.shape)]
        where[longest] = (where[longest] + shift) % result.shape[longest]
        spots.append(tuple(where))
    return result.at[spots[0]].set(low).at[spots[1]].set(high)


def block_levels(key, extent, cuts, low, high):
    loudness = 1.0
    for dim, parts in cuts:
        steps = jax.random.uniform(jax.random.fold_in(jax.random.fold_in(key, 6), dim), (parts,), jnp.float32, low / len(cuts), high / len(cuts))
        loudness = loudness * jnp.repeat(jnp.exp(steps), extent[dim] // parts).reshape((-1,) + (1,) * (len(extent) - 1 - dim))
    return loudness


def centred(own_key, extent, deviation, most, held_as=jnp.bfloat16):
    array = deviation * jax.random.normal(own_key, extent, jnp.float32)
    return jnp.clip(array, min=-most, max=most).astype(held_as)


def setup_inputs(seed: int = 0, part: int = 0) -> dict:
    keys = jax.random.split(jax.random.key(seed), 16)
    part_keys = jax.random.split(jax.random.fold_in(keys[15], part), 16)
    return {
        "positions": jnp.clip(1.0 * jax.random.uniform(part_keys[0], (3, DX, DY, DZ, A_DEV), jnp.float32) ** block_levels(part_keys[0], (3, DX, DY, DZ, A_DEV), ((1, 4), (2, 2), (3, 2)), -0.2, 0.2), 0.0, 1.0),
        "species": touch_ends(jax.random.randint(part_keys[1], (DX, DY, DZ, A_DEV), 0, SPECIES), jax.random.fold_in(part_keys[1], 1), 0, SPECIES - 1).astype(jnp.int32),
        "neighbours": draw_neighbours(jax.random.fold_in(jax.random.fold_in(keys[15], part), 71), part),
        "send_list": draw_send_list(jax.random.fold_in(jax.random.fold_in(keys[15], part), 71), part),
        "embedding": centred(keys[4], (SPECIES, C), 1.0, 6.0, jnp.float32),
        "radial_in": draw_radial_in(jax.random.fold_in(keys[15], 71), part),
        "radial_out_one": centred(keys[6], (RH, 2 * C), (16 * RH) ** -0.5, 0.1875, jnp.float32),
        "radial_in_two": draw_radial_in_two(jax.random.fold_in(keys[15], 71), part),
        "radial_out_two": centred(keys[8], (RH, 4 * C), (16 * RH) ** -0.5, 0.1875, jnp.float32),
        "mix_scalar_one": centred(keys[9], (C, C), C ** -0.5, 0.5, jnp.float32),
        "mix_square_one": centred(keys[10], (C, C), (4 * C) ** -0.5, 0.25, jnp.float32),
        "mix_vector_one": centred(keys[11], (C, C), C ** -0.5, 0.5, jnp.float32),
        "mix_scalar_two": centred(keys[12], (C, C), C ** -0.5, 0.5, jnp.float32),
        "mix_square_two": centred(keys[13], (C, C), (8 * C) ** -0.5, 0.1875, jnp.float32),
        "readout": centred(keys[14], (C,), (C // 4) ** -0.5, 1.0, jnp.float32),
    }


HIGHEST = lax.Precision.HIGHEST
MESSAGE_SCALE = 0.125
CUTOFF_SQUARED = 16.0
BLOCK_SLOTS = 16

def slot_offsets(ghost_count):
    slots = jnp.arange(27, dtype=jnp.int32)
    shifts = jnp.stack([slots // 9 - 1, slots // 3 % 3 - 1, slots % 3 - 1], axis=1).astype(jnp.float32)
    return jnp.repeat(shifts, ghost_count, axis=0)

def edge_terms(pos_own, pos_ext, slot_block, radial_first, radial_out):
    valid_mask = (slot_block >= 0).astype(jnp.float32)
    safe_index = jnp.maximum(slot_block, 0)
    relative = jnp.take(pos_ext, safe_index, axis=0) - pos_own[None, :, :]
    dist_sq = lax.optimization_barrier(jnp.sum(relative * relative, axis=-1))
    envelope = (1.0 - dist_sq / CUTOFF_SQUARED) ** 2 * valid_mask * MESSAGE_SCALE
    decay_rates = 0.08 * 2.0 ** (jnp.arange(radial_first.shape[0], dtype=jnp.float32) / 2.0)
    basis_values = jnp.exp(-dist_sq[..., None] * decay_rates)
    hidden = jax.nn.silu(jnp.einsum('kar,rh->kah', basis_values, radial_first, precision=HIGHEST))
    radial = jnp.einsum('kah,hp->kap', hidden, radial_out, precision=HIGHEST) * envelope[..., None]
    return (safe_index, relative, radial)

def layer_one(pos_own, pos_ext, species_ext, neighbours, embedding, radial_first, radial_out, mix_scalar, mix_square, mix_vector):
    channels = embedding.shape[1]
    atom_count = pos_own.shape[0]
    features = jnp.dot(species_ext, embedding, precision=HIGHEST)
    blocks = neighbours.reshape(-1, BLOCK_SLOTS, atom_count)

    def step_block(totals, slot_block):
        scalar_sum, vector_sum = totals
        safe_index, relative, radial = edge_terms(pos_own, pos_ext, slot_block, radial_first, radial_out)
        source = jnp.take(features, safe_index, axis=0)
        scalar_sum = scalar_sum + lax.optimization_barrier(jnp.sum(radial[..., :channels] * source, axis=0))
        vector_sum = vector_sum + jnp.einsum('kac,kax->xac', radial[..., channels:] * source, relative, precision=HIGHEST)
        return ((scalar_sum, vector_sum), None)
    initial = (jnp.zeros((atom_count, channels), jnp.float32), jnp.zeros((3, atom_count, channels), jnp.float32))
    (scalar_sum, vector_sum), unused = lax.scan(jax.checkpoint(step_block), initial, blocks)
    squares = lax.optimization_barrier(jnp.sum(vector_sum * vector_sum, axis=0))
    scalar_out = jax.nn.silu(jnp.dot(scalar_sum, mix_scalar, precision=HIGHEST) + jnp.dot(squares, mix_square, precision=HIGHEST))
    vector_out = jnp.einsum('xac,cd->xad', vector_sum, mix_vector, precision=HIGHEST)
    return jnp.concatenate([scalar_out[None], vector_out], axis=0)

def layer_two(pos_own, pos_ext, features_ext, neighbours, radial_first, radial_out, mix_scalar, mix_square, readout):
    channels = features_ext.shape[2]
    atom_count = pos_own.shape[0]
    blocks = neighbours.reshape(-1, BLOCK_SLOTS, atom_count)

    def step_block(totals, slot_block):
        scalar_sum, vector_sum = totals
        safe_index, relative, radial = edge_terms(pos_own, pos_ext, slot_block, radial_first, radial_out)
        source = jnp.take(features_ext, safe_index, axis=1)
        paths = radial.reshape(radial.shape[0], radial.shape[1], 4, channels)
        along = jnp.einsum('kax,xkac->kac', relative, source[1:], precision=HIGHEST)
        scalar_sum = scalar_sum + lax.optimization_barrier(jnp.sum(paths[:, :, 0] * source[0] + paths[:, :, 1] * along, axis=0))
        vector_sum = vector_sum + jnp.einsum('kac,kax->xac', paths[:, :, 2] * source[0], relative, precision=HIGHEST)
        vector_sum = vector_sum + lax.optimization_barrier(jnp.sum(paths[:, :, 3][None] * source[1:], axis=1))
        return ((scalar_sum, vector_sum), None)
    initial = (jnp.zeros((atom_count, channels), jnp.float32), jnp.zeros((3, atom_count, channels), jnp.float32))
    (scalar_sum, vector_sum), unused = lax.scan(jax.checkpoint(step_block), initial, blocks)
    squares = lax.optimization_barrier(jnp.sum(vector_sum * vector_sum, axis=0))
    mixed = jax.nn.silu(jnp.dot(scalar_sum, mix_scalar, precision=HIGHEST) + jnp.dot(squares, mix_square, precision=HIGHEST))
    return jnp.dot(mixed, readout, precision=HIGHEST)

def pick_rows(table, chosen):
    return table[chosen]

def pick_columns(table, chosen):
    return table[:, chosen]

def reference(positions, species, neighbours, send_list, embedding, radial_in, radial_out_one, radial_in_two, radial_out_two, mix_scalar_one, mix_square_one, mix_vector_one, mix_scalar_two, mix_square_two, readout):
    domains = DX * DY * DZ
    atom_pos = jnp.transpose(positions.reshape(3, domains, A_DEV), (1, 2, 0))
    species_flat = species.reshape(domains, A_DEV)
    neighbour_flat = neighbours.reshape(domains, NB, A_DEV)
    send_flat = send_list.reshape(domains, G_DEV)
    kinds = jnp.arange(SPECIES, dtype=jnp.int32)
    onehot = (species_flat[..., None] == kinds).astype(jnp.float32)
    domain_ids = jnp.arange(domains, dtype=jnp.int32)
    coord_x = domain_ids // (DY * DZ)
    coord_y = domain_ids // DZ % DY
    coord_z = domain_ids % DZ
    slots = jnp.arange(27, dtype=jnp.int32)
    nearby = ((coord_x[:, None] + slots // 9 - 1) % DX * (DY * DZ) + (coord_y[:, None] + slots // 3 % 3 - 1) % DY * DZ + (coord_z[:, None] + slots % 3 - 1) % DZ).astype(jnp.int32)
    offsets = slot_offsets(G_DEV)
    picked_species = jax.vmap(pick_rows)(onehot, send_flat)

    def total_energy(atom_pos):
        picked_pos = jax.vmap(pick_rows)(atom_pos, send_flat)

        def first(domain):
            own = atom_pos[domain]
            pos_ext = jnp.concatenate([own, picked_pos[nearby[domain]].reshape(27 * G_DEV, 3) + offsets], axis=0)
            species_ext = jnp.concatenate([onehot[domain], picked_species[nearby[domain]].reshape(27 * G_DEV, SPECIES)], axis=0)
            return layer_one(own, pos_ext, species_ext, neighbour_flat[domain], embedding, radial_in, radial_out_one, mix_scalar_one, mix_square_one, mix_vector_one)
        hidden_one = lax.map(jax.checkpoint(first), domain_ids)
        picked_hidden = jax.vmap(pick_columns)(hidden_one, send_flat)

        def second(domain):
            own = atom_pos[domain]
            pos_ext = jnp.concatenate([own, picked_pos[nearby[domain]].reshape(27 * G_DEV, 3) + offsets], axis=0)
            ghost = jnp.transpose(picked_hidden[nearby[domain]], (1, 0, 2, 3)).reshape(4, 27 * G_DEV, C)
            features_ext = jnp.concatenate([hidden_one[domain], ghost], axis=1)
            return layer_two(own, pos_ext, features_ext, neighbour_flat[domain], radial_in_two, radial_out_two, mix_scalar_two, mix_square_two, readout)
        energies = lax.map(jax.checkpoint(second), domain_ids)
        return (jnp.sum(energies), energies)
    gradient, energies = jax.grad(total_energy, has_aux=True)(atom_pos)
    forces = -jnp.transpose(gradient, (2, 0, 1)).reshape(3, DX, DY, DZ, A_DEV)
    return (forces, energies.reshape(DX, DY, DZ, A_DEV))
```

```python
import functools
import itertools

import jax
import jax.numpy as jnp
from jax import lax
from jax.experimental import pallas as pl
from jax.experimental.pallas import tpu as pltpu
from jax.sharding import PartitionSpec as P

MESSAGE_SCALE = 0.125
CUTOFF_SQUARED = 16.0
AXES = ("gx", "gy", "gz")
LANES = 128
GHOSTS = 16
REACH = 5
VMEM_BYTES = 52 * 1024 * 1024
F32 = jnp.float32
BF16 = jnp.bfloat16


def window_size(count):
    return min(count, REACH)


def window_place(relative, base, count):
    if count > REACH:
        return relative + 2
    place = relative + base
    for _ in range(2):
        place = jnp.where(place < 0, place + count, place)
    for _ in range(2):
        place = jnp.where(place >= count, place - count, place)
    return place


def near_steps(count):
    return [0, 1, -1][: min(count, 3)]


def near_place(step, count):
    if count >= 3:
        return jnp.where(step < 0, step + 3, step)
    return jnp.where(step == 0, 0, 1)


def split(x):
    high = x.astype(BF16)
    return high, (x - high.astype(F32)).astype(BF16)


def split_wide(x):
    high = x.astype(BF16).astype(F32)
    return high, x - high


def weight_stack(w):
    high, low = split(w)
    return jnp.concatenate([high, low, high], axis=0)


def data_stack(x):
    high, low = split(x)
    return jnp.concatenate([high, high, low], axis=0)


def dot_nn(a, b):
    return lax.dot_general(a, b, (((1,), (0,)), ((), ())), preferred_element_type=F32)


def dot_tn(a, b):
    return lax.dot_general(a, b, (((0,), (0,)), ((), ())), preferred_element_type=F32)


def dot_nt(a, b):
    return lax.dot_general(a, b, (((1,), (1,)), ((), ())), preferred_element_type=F32)


def product_nn(w_high, w_low, x):
    high, low = split(x)
    return dot_nn(w_high, high) + dot_nn(w_low, high) + dot_nn(w_high, low)


def sigmoid(v):
    return 1.0 / (1.0 + jnp.exp(-v))


def pick_lanes(row, index):
    return jnp.take_along_axis(jnp.broadcast_to(row, index.shape), index, axis=1)


def iota(shape, dim):
    return lax.broadcasted_iota(jnp.int32, shape, dim)


def pack_kernel(copies, send_ref, pos_ref, species_ref, neigh_ref, out_ref):
    lane = iota((8, LANES), 1)
    row = iota((8, LANES), 0)
    sent = jnp.zeros((8, LANES), jnp.int32)
    for s in range(GHOSTS):
        sent = jnp.where((lane & (GHOSTS - 1)) == s, send_ref[0, 0, 0, s], sent)
    block = jnp.zeros((8, LANES), F32)
    for x in range(3):
        block = jnp.where(row == x, pos_ref[x, 0, 0], block)
    block = jnp.where(row == 3, species_ref[0, 0].astype(F32), block)
    neigh = neigh_ref[0, 0, 0]
    for half in range(2):
        lists = jnp.take_along_axis(neigh[half * 8 : half * 8 + 8], sent, axis=1).astype(F32)
        kept = jnp.where((lane >> 4) == row, lists, 0.0)
        block = jnp.where(row == 4 + half, jnp.sum(kept, axis=0, keepdims=True), block)
    block = jnp.where(row == 6, sent.astype(F32), block)
    for w in range(copies):
        out_ref[w] = block


def forces_kernel(count, send_ref, parts_ref, out_ref):
    total = parts_ref[0]
    for w in range(1, count):
        total = total + parts_ref[w]
    lane = iota((8, LANES), 1)
    slot = jnp.full((8, LANES), -1, jnp.int32)
    for s in range(GHOSTS):
        slot = jnp.where(lane == send_ref[0, 0, 0, s], s, slot)
    moved = jnp.take_along_axis(total, jnp.maximum(slot, 0), axis=1)
    moved = jnp.where(slot >= 0, moved, 0.0)
    for x in range(3):
        out_ref[x, 0, 0] = -(total[x : x + 1] + moved[4 + x : 5 + x])


def main_kernel(
    dims,
    near,
    base_ref,
    table_ref,
    neigh_ref,
    embedding_ref,
    win_one_ref,
    wout_one_ref,
    win_two_ref,
    wout_two_ref,
    mss_one_ref,
    msq_one_ref,
    mv_one_ref,
    mss_two_ref,
    msq_two_ref,
    readout_ref,
    grad_ref,
    energy_ref,
    r_ref,
    kind_ref,
    dist_ref,
    wh_ref,
    slope_ref,
    wh2_ref,
    slope2_ref,
    moment_ref,
    pair_ref,
    target_ref,
    feat_ref,
    source_ref,
    radial_ref,
    node_ref,
    dsource_ref,
    dradial_ref,
    dr_ref,
    dmoment_ref,
):
    nx, ny, nz = dims
    wsize = tuple(window_size(n) for n in dims)
    windows = wsize[0] * wsize[1] * wsize[2]
    halves = -(-windows * GHOSTS // LANES)
    groups = 1 + -(-len(near) // 8)
    channels = LANES
    kinds = embedding_ref.shape[0]
    hidden = win_one_ref.shape[1]
    basis = win_one_ref.shape[0]
    own_edges = 16 * LANES
    atoms = groups * LANES

    lane16 = iota((16, LANES), 1)
    sub16 = iota((16, LANES), 0)
    lane8 = iota((8, LANES), 1)
    sub8 = iota((8, LANES), 0)
    bases = [base_ref[a] for a in range(3)]
    near_sizes = [len(near_steps(n)) for n in dims]

    def flat(steps):
        places = [window_place(steps[a], bases[a], dims[a]) for a in range(3)]
        return (places[0] * wsize[1] + places[1]) * wsize[2] + places[2]

    own_place = flat((0, 0, 0))
    near_places = [flat(step) for step in near]

    sent = [jnp.zeros((8, LANES), F32) for _ in range(halves)]
    for w in range(windows):
        block = table_ref[w]
        index = jnp.broadcast_to(block[6:7], (8, LANES)).astype(jnp.int32)
        picked = jnp.take_along_axis(block, index, axis=1)
        sent[w // 8] = jnp.where((lane8 >> 4) == w % 8, picked, sent[w // 8])

    for g in range(groups):
        members = [] if g == 0 else list(range((g - 1) * 8, min(g * 8, len(near))))
        if g == 0:
            entries = neigh_ref[0, 0, 0]
            own_block = table_ref[own_place]
            centre = [own_block[x : x + 1] for x in range(3)]
            steps = [0, 0, 0]
        else:
            centre8 = jnp.zeros((8, LANES), F32)
            listed = [jnp.full((8, LANES), -1.0, F32) for _ in range(2)]
            steps = [jnp.zeros((16, LANES), jnp.int32) for _ in range(3)]
            for q in members:
                block = table_ref[near_places[q]]
                here = (lane8 >> 4) == q % 8
                index = jnp.broadcast_to(block[6:7], (8, LANES)).astype(jnp.int32)
                centre8 = jnp.where(here, jnp.take_along_axis(block, index, axis=1), centre8)
                for half in range(2):
                    rows = pick_lanes(block[4 + half : 5 + half], sub8 * 16 + (lane8 & 15))
                    listed[half] = jnp.where(here, rows, listed[half])
                for a in range(3):
                    if near[q][a]:
                        steps[a] = jnp.where((lane16 >> 4) == q % 8, near[q][a], steps[a])
            entries = jnp.concatenate(listed, axis=0).astype(jnp.int32)
            centre = [centre8[x : x + 1] for x in range(3)]
        valid = entries >= 0
        named = jnp.maximum(entries, 0)
        local = named < LANES
        local_index = jnp.where(local, named, 0)
        ghost = jnp.maximum(named - LANES, 0)
        block_id, slot = ghost >> 4, ghost & 15
        first = (block_id * 57) >> 9
        rest = block_id - first * 9
        second = (rest * 11) >> 5
        shift = [first - 1, second - 1, rest - second * 3 - 1]
        sent_index = flat([shift[a] + steps[a] for a in range(3)]) * GHOSTS + slot
        values = []
        for x in range(4):
            if g == 0:
                inside = pick_lanes(own_block[x : x + 1], local_index)
            else:
                inside = jnp.zeros((16, LANES), F32)
                for q in members:
                    rows = pick_lanes(table_ref[near_places[q], x : x + 1, :], local_index)
                    inside = jnp.where((lane16 >> 4) == q % 8, rows, inside)
            outside = jnp.zeros((16, LANES), F32)
            for h in range(halves):
                rows = pick_lanes(sent[h][x : x + 1], sent_index & (LANES - 1))
                outside = jnp.where((sent_index >> 7) == h, rows, outside)
            if x < 3:
                outside = outside + shift[x].astype(F32)
            values.append(jnp.where(local, inside, outside))
        relative = [values[x] - centre[x] for x in range(3)]
        square = relative[0] * relative[0] + relative[1] * relative[1] + relative[2] * relative[2]
        linear = 1.0 - square / CUTOFF_SQUARED
        scale = jnp.where(valid, MESSAGE_SCALE, 0.0)
        dist_ref[0, g * 16 : g * 16 + 16, :] = square
        dist_ref[1, g * 16 : g * 16 + 16, :] = linear * linear * scale
        dist_ref[2, g * 16 : g * 16 + 16, :] = linear * scale * (-2.0 / CUTOFF_SQUARED)
        for n in range(16):
            for x in range(3):
                r_ref[x, g * 16 + n] = jnp.broadcast_to(relative[x][n : n + 1], (8, LANES))
            kind_ref[g * 16 + n] = jnp.broadcast_to(values[3][n : n + 1], (8, LANES))
        if g == 0:
            steps_near = [near_place(shift[a], dims[a]) for a in range(3)]
            order = (steps_near[0] * near_sizes[1] + steps_near[1]) * near_sizes[2] + steps_near[2]
            row = jnp.where(local, local_index, LANES + (order - 1) * GHOSTS + slot)
            size = atoms
        else:
            row = jnp.where(local, local_index, LANES + sent_index)
            size = LANES + halves * LANES
        row = jnp.where(valid, row, -1)
        position = iota((size, LANES), 0)
        for n in range(16):
            hot = jnp.where(position == row[n : n + 1], 1.0, 0.0).astype(BF16)
            if g == 0:
                pair_ref[0:size, n * LANES : (n + 1) * LANES] = hot
                pair_ref[size : 2 * size, n * LANES : (n + 1) * LANES] = hot
            else:
                target_ref[g - 1, :, n * LANES : (n + 1) * LANES] = hot

    rates = jnp.zeros((basis, LANES), F32)
    basis_row = iota((basis, LANES), 0)
    for m in range(basis):
        rates = jnp.where(basis_row == m, 0.08 * 2.0 ** (m / 2.0), rates)

    def radial_weights(win_ref):
        win = win_ref[...]
        both = jnp.concatenate([win, -rates[:, :hidden] * win], axis=1)
        high, low = split_wide(both)
        return jnp.concatenate([high, high, low, low], axis=0).astype(BF16)

    def radial_rows(weights, octet):
        dist8 = dist_ref[0, pl.ds(octet * 8, 8), :]
        weight8 = dist_ref[1, pl.ds(octet * 8, 8), :]
        slope8 = dist_ref[2, pl.ds(octet * 8, 8), :]
        values = jnp.concatenate([jnp.exp(-rates * dist8[j : j + 1]) for j in range(8)], axis=1)
        high, low = split_wide(values)
        stacked = jnp.concatenate([high, low, high, low], axis=0).astype(BF16)
        both = dot_tn(weights, stacked)
        rows = []
        for j in range(8):
            before = both[:hidden, j * LANES : (j + 1) * LANES]
            change = both[hidden:, j * LANES : (j + 1) * LANES]
            gate = sigmoid(before)
            after = before * gate
            gain = gate * (1.0 + before * (1.0 - gate))
            weight = weight8[j : j + 1]
            rows.append((weight * after, slope8[j : j + 1] * after + weight * (gain * change)))
        return rows

    weights_one = radial_weights(win_one_ref)
    weights_two = radial_weights(win_two_ref)

    def radial_one_step(octet, carry):
        for j, (value, slope) in enumerate(radial_rows(weights_one, octet)):
            wh_ref[octet * 8 + j] = value
            slope_ref[octet * 8 + j] = slope
        return carry

    lax.fori_loop(0, groups * 2, radial_one_step, 0)

    def radial_two_step(octet, carry):
        rows = radial_rows(weights_two, octet)
        lanes = pl.ds(pl.multiple_of(octet * 8 * LANES, 8 * LANES), 8 * LANES)
        stack = data_stack(jnp.concatenate([value for value, _ in rows], axis=1))
        wh2_ref[:, lanes] = stack
        for j, (_, slope) in enumerate(rows):
            slope2_ref[octet * 8 + j] = slope
        return carry

    lax.fori_loop(0, 2, radial_two_step, 0)

    def moment_step(step, carry):
        g, part = step // (hidden // 8), step % (hidden // 8)
        rows = pl.ds(pl.multiple_of(part * 8, 8), 8)
        lanes = pl.ds(pl.multiple_of(g * LANES, LANES), LANES)
        sums = [[jnp.zeros((8, LANES), F32) for _ in range(4)] for _ in range(kinds)]
        for n in range(16):
            e = g * 16 + n
            value = wh_ref[e, rows, :]
            parts = [value] + [value * r_ref[x, e] for x in range(3)]
            kind = kind_ref[e]
            for s in range(kinds):
                mask = kind == float(s)
                for j in range(4):
                    sums[s][j] = sums[s][j] + jnp.where(mask, parts[j], 0.0)
        for s in range(kinds):
            for j in range(4):
                place = pl.ds(pl.multiple_of(s * hidden + part * 8, 8), 8)
                moment_ref[j, place, lanes] = sums[s][j]
        return carry

    lax.fori_loop(0, groups * (hidden // 8), moment_step, 0)

    wout_one = wout_one_ref[...]
    combined = []
    for j in range(2):
        columns = wout_one[:, j * channels : (j + 1) * channels]
        rows = [columns * embedding_ref[s : s + 1, :] for s in range(kinds)]
        combined.append(jnp.concatenate(rows, axis=0))
    stacked_weights = [weight_stack(w) for w in combined]
    scalar_one = dot_tn(stacked_weights[0], data_stack(moment_ref[0]))
    vector_one = [dot_tn(stacked_weights[1], data_stack(moment_ref[1 + x])) for x in range(3)]
    squares_one = sum(v * v for v in vector_one)
    mss_one, msq_one, mv_one = mss_one_ref[...], msq_one_ref[...], mv_one_ref[...]
    mix_one = jnp.concatenate([weight_stack(mss_one), weight_stack(msq_one)], axis=0)
    before_one = dot_tn(
        mix_one, jnp.concatenate([data_stack(scalar_one), data_stack(squares_one)], axis=0)
    )
    gate_one = sigmoid(before_one)
    mv_stack = weight_stack(mv_one)
    features = [before_one * gate_one] + [dot_tn(mv_stack, data_stack(v)) for v in vector_one]
    gain_one = gate_one * (1.0 + before_one * (1.0 - gate_one))
    for j in range(4):
        rows = slice(j * channels, (j + 1) * channels)
        feat_ref[rows, 0:atoms], feat_ref[rows, atoms : 2 * atoms] = split(features[j])
    node_ref[4, :, 0:atoms] = gain_one
    for x in range(3):
        node_ref[5 + x, :, 0:atoms] = vector_one[x]

    wout_two = wout_two_ref[...]
    wout_two_high, wout_two_low = split(wout_two)
    radial_stack = jnp.concatenate([wout_two_high, wout_two_low, wout_two_high], axis=0)

    def edge_step(step, carry):
        lanes = pl.ds(pl.multiple_of(step * 256, 256), 256)
        source_ref[:, lanes] = dot_nn(feat_ref[...], pair_ref[:, lanes])
        radial_ref[:, lanes] = dot_tn(radial_stack, wh2_ref[:, lanes])
        return carry

    lax.fori_loop(0, own_edges // 256, edge_step, 0)

    def sum_step(part, carry):
        def rows(j):
            return pl.ds(pl.multiple_of(j * channels + part * 8, 8), 8)

        sums = [jnp.zeros((8, LANES), F32) for _ in range(4)]
        for n in range(16):
            lanes = slice(n * LANES, (n + 1) * LANES)
            t = source_ref[rows(0), lanes]
            u = [source_ref[rows(1 + x), lanes] for x in range(3)]
            paths = [radial_ref[rows(j), lanes] for j in range(4)]
            r = [r_ref[x, n] for x in range(3)]
            along = r[0] * u[0] + r[1] * u[1] + r[2] * u[2]
            sums[0] = sums[0] + (paths[0] * t + paths[1] * along)
            turned = paths[2] * t
            for x in range(3):
                sums[1 + x] = sums[1 + x] + (turned * r[x] + paths[3] * u[x])
        for j in range(4):
            node_ref[j, pl.ds(pl.multiple_of(part * 8, 8), 8), 0:LANES] = sums[j]
        return carry

    lax.fori_loop(0, channels // 8, sum_step, 0)

    scalar_two = node_ref[0, :, 0:LANES]
    vector_two = [node_ref[1 + x, :, 0:LANES] for x in range(3)]
    squares_two = sum(v * v for v in vector_two)
    mss_two, msq_two = mss_two_ref[...], msq_two_ref[...]
    mix_two = jnp.concatenate([weight_stack(mss_two), weight_stack(msq_two)], axis=0)
    before_two = dot_tn(
        mix_two, jnp.concatenate([data_stack(scalar_two), data_stack(squares_two)], axis=0)
    )
    gate_two = sigmoid(before_two)
    readout = jnp.transpose(jnp.broadcast_to(readout_ref[...], (LANES, channels)))
    energy_ref[0, 0] = jnp.sum(readout * (before_two * gate_two), axis=0, keepdims=True)
    dbefore_two = readout * (gate_two * (1.0 + before_two * (1.0 - gate_two)))
    dscalar_two = product_nn(*split(mss_two), dbefore_two)
    dsquares_two = product_nn(*split(msq_two), dbefore_two)
    node_ref[0, :, 0:LANES] = dscalar_two
    for x in range(3):
        node_ref[1 + x, :, 0:LANES] = 2.0 * vector_two[x] * dsquares_two

    def back_step(n, carry):
        lanes = pl.ds(pl.multiple_of(n * LANES, LANES), LANES)
        r = [jnp.concatenate([r_ref[x, n]] * 2, axis=0) for x in range(3)]
        totals = [jnp.zeros((16, LANES), F32) for _ in range(3)]
        for part in range(channels // 16):

            def rows(j):
                return slice(j * channels + part * 16, j * channels + part * 16 + 16)

            t = source_ref[rows(0), lanes]
            u = [source_ref[rows(1 + x), lanes] for x in range(3)]
            paths = [radial_ref[rows(j), lanes] for j in range(4)]
            ds = node_ref[0, rows(0), 0:LANES]
            dv = [node_ref[1 + x, rows(0), 0:LANES] for x in range(3)]
            push = paths[1] * ds
            facing = r[0] * dv[0] + r[1] * dv[1] + r[2] * dv[2]
            along = r[0] * u[0] + r[1] * u[1] + r[2] * u[2]
            meeting = dv[0] * u[0] + dv[1] * u[1] + dv[2] * u[2]
            turned = paths[2] * t
            dsource = [paths[0] * ds + paths[2] * facing]
            for x in range(3):
                dsource.append(push * r[x] + paths[3] * dv[x])
                totals[x] = totals[x] + (push * u[x] + turned * dv[x])
            dradial = [ds * t, ds * along, t * facing, meeting]
            for j in range(4):
                dsource_ref[0, rows(j), lanes], dsource_ref[1, rows(j), lanes] = split(dsource[j])
                dradial_ref[0, rows(j), lanes], dradial_ref[1, rows(j), lanes] = split(dradial[j])
        for x in range(3):
            total = jnp.sum(totals[x], axis=0, keepdims=True)
            dr_ref[x : x + 1, lanes] = total
        return carry

    lax.fori_loop(0, 16, back_step, 0)

    dfeat = dot_nt(dsource_ref[0], pair_ref[0:atoms, :]) + dot_nt(
        dsource_ref[1], pair_ref[0:atoms, :]
    )

    def radial_back_step(step, carry):
        lanes = pl.ds(pl.multiple_of(step * 512, 512), 512)
        dhigh, dlow = dradial_ref[0, :, lanes], dradial_ref[1, :, lanes]
        dwh = dot_nn(wout_two_high, dhigh) + dot_nn(wout_two_low, dhigh) + dot_nn(wout_two_high, dlow)
        for j in range(4):
            n = step * 4 + j
            dd = jnp.sum(
                dwh[:, j * LANES : (j + 1) * LANES] * slope2_ref[n], axis=0, keepdims=True
            )
            at = pl.ds(pl.multiple_of(n * LANES, LANES), LANES)
            for x in range(3):
                dr_ref[x : x + 1, at] = dr_ref[x : x + 1, at] + 2.0 * dd * r_ref[x, n, 0:1, :]
        return carry

    lax.fori_loop(0, 4, radial_back_step, 0)

    gain_one = node_ref[4, :, 0:atoms]
    vector_one = [node_ref[5 + x, :, 0:atoms] for x in range(3)]
    dbefore_one = dfeat[0:channels] * gain_one
    dscalar_one = product_nn(*split(mss_one), dbefore_one)
    dsquares_one = product_nn(*split(msq_one), dbefore_one)
    mv_parts = split(mv_one)
    dmoment_ref[0] = product_nn(*split(combined[0]), dscalar_one)
    combined_parts = split(combined[1])
    for x in range(3):
        du = dfeat[(1 + x) * channels : (2 + x) * channels]
        dvector = 2.0 * vector_one[x] * dsquares_one + product_nn(*mv_parts, du)
        dmoment_ref[1 + x] = product_nn(*combined_parts, dvector)

    def one_back_step(step, carry):
        g = step // 4
        lanes = pl.ds(pl.multiple_of(g * LANES, LANES), LANES)
        edges = [step * 4 + j for j in range(4)]
        totals = [[jnp.zeros((8, LANES), F32) for _ in range(4)] for _ in range(4)]
        for part in range(hidden // 8):
            rows = slice(part * 8, part * 8 + 8)
            pulls = [
                [dmoment_ref[m, s * hidden + part * 8 : s * hidden + part * 8 + 8, lanes] for m in range(4)]
                for s in range(kinds)
            ]
            for j, e in enumerate(edges):
                kind = kind_ref[e]
                chosen = pulls[0]
                for s in range(1, kinds):
                    mask = kind == float(s)
                    chosen = [jnp.where(mask, pulls[s][m], chosen[m]) for m in range(4)]
                r = [r_ref[x, e] for x in range(3)]
                dwh = chosen[0] + r[0] * chosen[1] + r[1] * chosen[2] + r[2] * chosen[3]
                value = wh_ref[e, rows, :]
                totals[j][3] = totals[j][3] + dwh * slope_ref[e, rows, :]
                for x in range(3):
                    totals[j][x] = totals[j][x] + value * chosen[1 + x]
        for j, e in enumerate(edges):
            at = pl.ds(pl.multiple_of(e * LANES, LANES), LANES)
            dd = 2.0 * jnp.sum(totals[j][3], axis=0, keepdims=True)
            for x in range(3):
                change = jnp.sum(totals[j][x], axis=0, keepdims=True) + dd * r_ref[x, e, 0:1, :]
                dr_ref[4 + x : 5 + x, at] = change
        return carry

    lax.fori_loop(0, groups * 4, one_back_step, 0)

    pieces = []
    for e in range(groups * 16):
        at = slice(e * LANES, (e + 1) * LANES)
        piece = dr_ref[:, at]
        low = pltpu.roll(piece, 4, 0)
        if e < 16:
            piece = jnp.where((sub8 & 3) == 3, 0.0, piece + low)
        else:
            piece = jnp.where((sub8 & 3) == 3, 0.0, jnp.where(sub8 < 4, low, piece))
        pieces.append(piece)
    centres = [sum(pieces[g * 16 : g * 16 + 16]) for g in range(groups)]
    own_change = jnp.concatenate(pieces[:16], axis=1)
    own_high, own_low = split_wide(own_change)
    moved = dot_nt(jnp.concatenate([own_high, own_low], axis=0).astype(BF16), pair_ref[0:atoms, :])
    moved = moved[0:8] + moved[8:16]
    moved = [moved[:, g * LANES : (g + 1) * LANES] - centres[g] for g in range(groups)]

    sent_totals = [jnp.zeros((8, LANES), F32) for _ in range(halves)]
    inner = {}
    for g in range(1, groups):
        members = range((g - 1) * 8, min(g * 8, len(near)))
        change = jnp.concatenate(pieces[g * 16 : g * 16 + 16], axis=1)
        high, low = split_wide(change)
        owner = (iota(change.shape, 1) & (LANES - 1)) >> 4
        stack = [high, low]
        for q in members:
            here = owner == q % 8
            stack += [jnp.where(here, high, 0.0), jnp.where(here, low, 0.0)]
        spread = dot_nt(jnp.concatenate(stack, axis=0).astype(BF16), target_ref[g - 1])
        for h in range(halves):
            lanes = slice(LANES + h * LANES, 2 * LANES + h * LANES)
            sent_totals[h] = sent_totals[h] + (spread[0:8, lanes] + spread[8:16, lanes])
        for i, q in enumerate(members):
            at = 16 + i * 16
            inner[q] = spread[at : at + 8, 0:LANES] + spread[at + 8 : at + 16, 0:LANES]

    spot = lane8 & 15
    for w in range(windows):
        block = jnp.take_along_axis(sent_totals[w // 8], (w % 8) * 16 + spot, axis=1)
        grad_ref[w] = jnp.where(sub8 < 4, 0.0, block)
    grad_ref[own_place] = grad_ref[own_place] + jnp.where(sub8 < 4, moved[0], 0.0)
    for q in range(len(near)):
        block = jnp.take_along_axis(moved[1 + q // 8], (q % 8) * 16 + spot, axis=1)
        grad_ref[near_places[q]] = grad_ref[near_places[q]] + jnp.where(sub8 < 4, inner[q], block)


def send_along(value, axis, steps):
    count = lax.axis_size(axis)
    return lax.ppermute(value, axis, [(i, (i + steps) % count) for i in range(count)])


def axis_steps(count):
    return list(range(count)) if count <= REACH else list(range(-2, 3))


def per_device(
    positions,
    species,
    neighbours,
    send_list,
    embedding,
    radial_in,
    radial_out_one,
    radial_in_two,
    radial_out_two,
    mix_scalar_one,
    mix_square_one,
    mix_vector_one,
    mix_scalar_two,
    mix_square_two,
    readout,
):
    dims = tuple(lax.axis_size(axis) for axis in AXES)
    windows = 1
    for count in dims:
        windows *= window_size(count)
    whole = windows == dims[0] * dims[1] * dims[2] and windows <= 16
    near = [step for step in itertools.product(*[near_steps(n) for n in dims])][1:]
    groups = 1 + -(-len(near) // 8)
    halves = -(-windows * GHOSTS // LANES)
    atoms = groups * LANES
    hidden = radial_in.shape[1]
    kinds, channels = embedding.shape
    copies = windows if whole else 1
    smem = pl.BlockSpec(memory_space=pltpu.SMEM)
    vmem = pl.BlockSpec(memory_space=pltpu.VMEM)

    packed = pl.pallas_call(
        functools.partial(pack_kernel, copies),
        out_shape=jax.ShapeDtypeStruct((copies, 8, LANES), F32),
        in_specs=[smem, vmem, vmem, vmem],
        out_specs=vmem,
    )(send_list, positions, species, neighbours)

    if whole:
        table = lax.all_to_all(packed, AXES, 0, 0, tiled=True)
        base = jnp.stack([lax.axis_index(axis) for axis in AXES]).astype(jnp.int32)
    else:
        table = packed.reshape(1, 1, 1, 8, LANES)
        for dim, axis in reversed(list(enumerate(AXES))):
            parts = [
                send_along(table, axis, -step) if step else table for step in axis_steps(dims[dim])
            ]
            table = jnp.concatenate(parts, axis=dim)
        table = table.reshape(windows, 8, LANES)
        base = jnp.zeros((3,), jnp.int32)

    rows = groups * 16
    edges = 16 * LANES
    grads, energy = pl.pallas_call(
        functools.partial(main_kernel, dims, near),
        out_shape=(
            jax.ShapeDtypeStruct((windows, 8, LANES), F32),
            jax.ShapeDtypeStruct((1, 1, 1, LANES), F32),
        ),
        in_specs=[smem] + [vmem] * 13,
        out_specs=(vmem, vmem),
        scratch_shapes=[
            pltpu.VMEM((3, rows, 8, LANES), F32),
            pltpu.VMEM((rows, 8, LANES), F32),
            pltpu.VMEM((3, rows, LANES), F32),
            pltpu.VMEM((rows, hidden, LANES), F32),
            pltpu.VMEM((rows, hidden, LANES), F32),
            pltpu.VMEM((3 * hidden, edges), BF16),
            pltpu.VMEM((16, hidden, LANES), F32),
            pltpu.VMEM((4, kinds * hidden, atoms), F32),
            pltpu.VMEM((2 * atoms, edges), BF16),
            pltpu.VMEM((groups - 1, LANES + halves * LANES, edges), BF16),
            pltpu.VMEM((4 * channels, 2 * atoms), BF16),
            pltpu.VMEM((4 * channels, edges), F32),
            pltpu.VMEM((4 * channels, edges), F32),
            pltpu.VMEM((8, channels, atoms), F32),
            pltpu.VMEM((2, 4 * channels, edges), BF16),
            pltpu.VMEM((2, 4 * channels, edges), BF16),
            pltpu.VMEM((8, rows * LANES), F32),
            pltpu.VMEM((4, kinds * hidden, atoms), F32),
        ],
        compiler_params=pltpu.CompilerParams(vmem_limit_bytes=VMEM_BYTES),
    )(
        base,
        table,
        neighbours,
        embedding,
        radial_in,
        radial_out_one,
        radial_in_two,
        radial_out_two,
        mix_scalar_one,
        mix_square_one,
        mix_vector_one,
        mix_scalar_two,
        mix_square_two,
        readout.reshape(1, channels),
    )

    if whole:
        returned = lax.all_to_all(grads, AXES, 0, 0, tiled=True)
    else:
        returned = grads.reshape(tuple(window_size(n) for n in dims) + (8, LANES))
        for dim, axis in enumerate(AXES):
            total = None
            for place, step in enumerate(axis_steps(dims[dim])):
                part = lax.slice_in_dim(returned, place, place + 1, axis=dim)
                part = send_along(part, axis, step) if step else part
                total = part if total is None else total + part
            returned = total
        returned = returned.reshape(1, 8, LANES)

    forces = pl.pallas_call(
        functools.partial(forces_kernel, copies),
        out_shape=jax.ShapeDtypeStruct((3, 1, 1, 1, LANES), F32),
        in_specs=[smem, vmem],
        out_specs=vmem,
    )(send_list, returned)
    return (forces.reshape(3, 1, 1, 1, LANES), energy)


def solution(mesh):
    spread = ("groups", "gx")
    return jax.shard_map(
        per_device,
        mesh=mesh,
        in_specs=(
            P(None, spread, "gy", "gz", None),
            P(spread, "gy", "gz", None),
            P(spread, "gy", "gz", None, None),
            P(spread, "gy", "gz", None),
        )
        + (P(),) * 11,
        out_specs=(P(None, spread, "gy", "gz", None), P(spread, "gy", "gz", None)),
        check_vma=False,
    )
```

```python
import functools
import itertools

import jax
import jax.numpy as jnp
from jax import lax
from jax.experimental import pallas as pl
from jax.experimental.pallas import tpu as pltpu
from jax.sharding import PartitionSpec as P

MESSAGE_SCALE = 0.125
CUTOFF_SQUARED = 16.0
AXES = ("gx", "gy", "gz")
LANES = 128
GHOSTS = 16
REACH = 5
VMEM_BYTES = 60 * 1024 * 1024
F32 = jnp.float32
BF16 = jnp.bfloat16


def window_size(count):
    return min(count, REACH)


def window_place(relative, base, count):
    if count > REACH:
        return relative + 2
    place = relative + base
    for _ in range(2):
        place = jnp.where(place < 0, place + count, place)
    for _ in range(2):
        place = jnp.where(place >= count, place - count, place)
    return place


def near_steps(count):
    return [0, 1, -1][: min(count, 3)]


def near_place(step, count):
    if count >= 3:
        return jnp.where(step < 0, step + 3, step)
    return jnp.where(step == 0, 0, 1)


def split(x):
    high = x.astype(BF16)
    return high, (x - high.astype(F32)).astype(BF16)


def split_wide(x):
    high = x.astype(BF16).astype(F32)
    return high, x - high


def weight_stack(w):
    high, low = split(w)
    return jnp.concatenate([high, low, high], axis=0)


def data_stack(x):
    high, low = split(x)
    return jnp.concatenate([high, high, low], axis=0)


def dot_nn(a, b):
    return lax.dot_general(a, b, (((1,), (0,)), ((), ())), preferred_element_type=F32)


def dot_tn(a, b):
    return lax.dot_general(a, b, (((0,), (0,)), ((), ())), preferred_element_type=F32)


def dot_nt(a, b):
    return lax.dot_general(a, b, (((1,), (1,)), ((), ())), preferred_element_type=F32)


def product_nn(w_high, w_low, x):
    high, low = split(x)
    return dot_nn(w_high, high) + dot_nn(w_low, high) + dot_nn(w_high, low)


def sigmoid(v):
    return 0.5 + 0.5 * jnp.tanh(0.5 * v)


def pick_lanes(row, index):
    return jnp.take_along_axis(jnp.broadcast_to(row, index.shape), index, axis=1)


def iota(shape, dim):
    return lax.broadcasted_iota(jnp.int32, shape, dim)


def pack_kernel(copies, send_ref, pos_ref, species_ref, neigh_ref, out_ref):
    lane = iota((8, LANES), 1)
    row = iota((8, LANES), 0)
    sent = jnp.zeros((8, LANES), jnp.int32)
    for s in range(GHOSTS):
        sent = jnp.where((lane & (GHOSTS - 1)) == s, send_ref[0, 0, 0, s], sent)
    block = jnp.zeros((8, LANES), F32)
    for x in range(3):
        block = jnp.where(row == x, pos_ref[x, 0, 0], block)
    block = jnp.where(row == 3, species_ref[0, 0].astype(F32), block)
    neigh = neigh_ref[0, 0, 0]
    for half in range(2):
        lists = jnp.take_along_axis(neigh[half * 8 : half * 8 + 8], sent, axis=1).astype(F32)
        kept = jnp.where((lane >> 4) == row, lists, 0.0)
        block = jnp.where(row == 4 + half, jnp.sum(kept, axis=0, keepdims=True), block)
    block = jnp.where(row == 6, sent.astype(F32), block)
    for w in range(copies):
        out_ref[w] = block


def forces_kernel(count, send_ref, parts_ref, out_ref):
    total = parts_ref[0]
    for w in range(1, count):
        total = total + parts_ref[w]
    lane = iota((8, LANES), 1)
    slot = jnp.full((8, LANES), -1, jnp.int32)
    for s in range(GHOSTS):
        slot = jnp.where(lane == send_ref[0, 0, 0, s], s, slot)
    moved = jnp.take_along_axis(total, jnp.maximum(slot, 0), axis=1)
    moved = jnp.where(slot >= 0, moved, 0.0)
    for x in range(3):
        out_ref[x, 0, 0] = -(total[x : x + 1] + moved[4 + x : 5 + x])


def decay_rates(basis):
    rates = jnp.zeros((basis, LANES), F32)
    row = iota((basis, LANES), 0)
    for m in range(basis):
        rates = jnp.where(row == m, 0.08 * 2.0 ** (m / 2.0), rates)
    return rates


def ghost_parts(named):
    ghost = jnp.maximum(named - LANES, 0)
    block_id, slot = ghost >> 4, ghost & 15
    first = (block_id * 57) >> 9
    rest = block_id - first * 9
    second = (rest * 11) >> 5
    return [first - 1, second - 1, rest - second * 3 - 1], slot


def wide_stack(w):
    high, low = split(w)
    return jnp.concatenate([high, low, high], axis=1)


def turned_stack(w):
    return wide_stack(jnp.transpose(w))


def prepare_kernel(
    dims,
    neigh_ref,
    embedding_ref,
    win_one_ref,
    wout_one_ref,
    win_two_ref,
    wout_two_ref,
    mss_one_ref,
    msq_one_ref,
    mv_one_ref,
    mss_two_ref,
    msq_two_ref,
    readout_ref,
    pair_ref,
    basis_ref,
    slots_ref,
    pulls_ref,
    mixes_ref,
    turns_ref,
    paths_ref,
    read_ref,
):
    atoms = pair_ref.shape[0]
    basis, hidden = win_one_ref.shape
    kinds, channels = embedding_ref.shape
    near_sizes = [len(near_steps(n)) for n in dims]
    entries = neigh_ref[0, 0, 0]
    named = jnp.maximum(entries, 0)
    shift, slot = ghost_parts(named)
    steps = [near_place(shift[a], dims[a]) for a in range(3)]
    order = (steps[0] * near_sizes[1] + steps[1]) * near_sizes[2] + steps[2]
    row = jnp.where(named < LANES, named, LANES + (order - 1) * GHOSTS + slot)
    row = jnp.where(entries >= 0, row, -1)
    position = iota((atoms, LANES), 0)
    for n in range(16):
        hot = jnp.where(position == row[n : n + 1], 1.0, 0.0).astype(BF16)
        pair_ref[:, n * LANES : (n + 1) * LANES] = hot

    rates = decay_rates(basis)
    for i, win_ref in enumerate((win_one_ref, win_two_ref)):
        win = win_ref[...]
        both = jnp.concatenate([win, -rates[:, :hidden] * win], axis=1)
        high, low = split_wide(both)
        basis_ref[i] = jnp.concatenate([high, high, low, low], axis=0).astype(BF16)
    for j in range(2):
        columns = wout_one_ref[:, j * channels : (j + 1) * channels]
        rows = [columns * embedding_ref[s : s + 1, :] for s in range(kinds)]
        combined = jnp.concatenate(rows, axis=0)
        high, low = split_wide(combined)
        slots_ref[j] = jnp.transpose(jnp.concatenate([high, low, high], axis=0)).astype(BF16)
        pulls_ref[j] = wide_stack(combined)
    pairs = ((mss_one_ref, msq_one_ref), (mss_two_ref, msq_two_ref))
    for i, (scalar_ref, square_ref) in enumerate(pairs):
        mixes_ref[i] = jnp.concatenate(
            [turned_stack(scalar_ref[...]), turned_stack(square_ref[...])], axis=1
        )
        turns_ref[2 + 2 * i] = wide_stack(scalar_ref[...])
        turns_ref[3 + 2 * i] = wide_stack(square_ref[...])
    turns_ref[0] = turned_stack(mv_one_ref[...])
    turns_ref[1] = wide_stack(mv_one_ref[...])
    high, low = split_wide(wout_two_ref[...])
    paths_ref[...] = jnp.transpose(jnp.concatenate([high, low, high], axis=0)).astype(BF16)
    read_ref[...] = jnp.transpose(jnp.broadcast_to(readout_ref[...], (LANES, channels)))


def main_kernel(
    dims,
    near,
    whole,
    table_ref,
    neigh_ref,
    pair_hbm,
    basis_hbm,
    slots_hbm,
    pulls_hbm,
    mixes_hbm,
    turns_hbm,
    paths_hbm,
    readout_hbm,
    grad_ref,
    energy_ref,
    r_ref,
    kind_ref,
    dist_ref,
    wh_ref,
    slope_ref,
    wh2_ref,
    moment_ref,
    target_ref,
    feat_ref,
    source_ref,
    radial_ref,
    node_ref,
    dsource_ref,
    dr_ref,
    dmoment_ref,
    pair_ref,
    basis_ref,
    slots_ref,
    pulls_ref,
    mixes_ref,
    turns_ref,
    paths_ref,
    readout_ref,
    copy_sem,
):
    atoms = pair_hbm.shape[0]
    moves = {}
    for i, (name, source, target) in enumerate(
        (
            ("basis", basis_hbm, basis_ref),
            ("slots", slots_hbm, slots_ref),
            ("mixes", mixes_hbm, mixes_ref),
            ("turns", turns_hbm, turns_ref),
            ("high", pair_hbm, pair_ref.at[0:atoms]),
            ("low", pair_hbm, pair_ref.at[atoms : 2 * atoms]),
            ("paths", paths_hbm, paths_ref),
            ("readout", readout_hbm, readout_ref),
            ("pulls", pulls_hbm, pulls_ref),
        )
    ):
        moves[name] = pltpu.make_async_copy(source, target, copy_sem.at[i])
        moves[name].start()

    def ready(*names):
        for name in names:
            moves.pop(name).wait()

    wsize = tuple(window_size(n) for n in dims)
    windows = wsize[0] * wsize[1] * wsize[2]
    halves = -(-windows * GHOSTS // LANES)
    groups = 1 + -(-len(near) // 8)
    channels = LANES
    hidden = paths_ref.shape[1] // 3
    kinds = pulls_ref.shape[1] // hidden
    basis = basis_ref.shape[1] // 4
    own_edges = 16 * LANES

    lane16 = iota((16, LANES), 1)
    sub16 = iota((16, LANES), 0)
    lane8 = iota((8, LANES), 1)
    sub8 = iota((8, LANES), 0)
    bases = [lax.axis_index(axis) if whole else 0 for axis in AXES]
    near_sizes = [len(near_steps(n)) for n in dims]

    def flat(steps):
        places = [window_place(steps[a], bases[a], dims[a]) for a in range(3)]
        return (places[0] * wsize[1] + places[1]) * wsize[2] + places[2]

    own_place = flat((0, 0, 0))
    near_places = [flat(step) for step in near]

    sent = [jnp.zeros((8, LANES), F32) for _ in range(halves)]
    for w in range(windows):
        block = table_ref[w]
        index = jnp.broadcast_to(block[6:7], (8, LANES)).astype(jnp.int32)
        picked = jnp.take_along_axis(block, index, axis=1)
        sent[w // 8] = jnp.where((lane8 >> 4) == w % 8, picked, sent[w // 8])

    for g in range(groups):
        members = [] if g == 0 else list(range((g - 1) * 8, min(g * 8, len(near))))
        if g == 0:
            entries = neigh_ref[0, 0, 0]
            own_block = table_ref[own_place]
            centre = [own_block[x : x + 1] for x in range(3)]
            steps = [0, 0, 0]
        else:
            centre8 = jnp.zeros((8, LANES), F32)
            listed = [jnp.full((8, LANES), -1.0, F32) for _ in range(2)]
            steps = [jnp.zeros((16, LANES), jnp.int32) for _ in range(3)]
            for q in members:
                block = table_ref[near_places[q]]
                here = (lane8 >> 4) == q % 8
                index = jnp.broadcast_to(block[6:7], (8, LANES)).astype(jnp.int32)
                centre8 = jnp.where(here, jnp.take_along_axis(block, index, axis=1), centre8)
                for half in range(2):
                    rows = pick_lanes(block[4 + half : 5 + half], sub8 * 16 + (lane8 & 15))
                    listed[half] = jnp.where(here, rows, listed[half])
                for a in range(3):
                    if near[q][a]:
                        steps[a] = jnp.where((lane16 >> 4) == q % 8, near[q][a], steps[a])
            entries = jnp.concatenate(listed, axis=0).astype(jnp.int32)
            centre = [centre8[x : x + 1] for x in range(3)]
        valid = entries >= 0
        named = jnp.maximum(entries, 0)
        local = named < LANES
        local_index = jnp.where(local, named, 0)
        shift, slot = ghost_parts(named)
        sent_index = flat([shift[a] + steps[a] for a in range(3)]) * GHOSTS + slot
        values = []
        for x in range(4):
            if g == 0:
                inside = pick_lanes(own_block[x : x + 1], local_index)
            else:
                inside = jnp.zeros((16, LANES), F32)
                for q in members:
                    rows = pick_lanes(table_ref[near_places[q], x : x + 1, :], local_index)
                    inside = jnp.where((lane16 >> 4) == q % 8, rows, inside)
            outside = jnp.zeros((16, LANES), F32)
            for h in range(halves):
                rows = pick_lanes(sent[h][x : x + 1], sent_index & (LANES - 1))
                outside = jnp.where((sent_index >> 7) == h, rows, outside)
            if x < 3:
                outside = outside + shift[x].astype(F32)
            values.append(jnp.where(local, inside, outside))
        relative = [values[x] - centre[x] for x in range(3)]
        square = relative[0] * relative[0] + relative[1] * relative[1] + relative[2] * relative[2]
        linear = 1.0 - square / CUTOFF_SQUARED
        scale = jnp.where(valid, MESSAGE_SCALE, 0.0)
        dist_ref[0, g * 16 : g * 16 + 16, :] = square
        dist_ref[1, g * 16 : g * 16 + 16, :] = linear * linear * scale
        dist_ref[2, g * 16 : g * 16 + 16, :] = linear * scale * (-2.0 / CUTOFF_SQUARED)
        for n in range(16):
            for x in range(3):
                r_ref[x, g * 16 + n] = jnp.broadcast_to(relative[x][n : n + 1], (8, LANES))
            kind_ref[g * 16 + n] = jnp.broadcast_to(values[3][n : n + 1], (8, LANES))
        if g == 0:
            continue
        row = jnp.where(local, local_index, LANES + sent_index)
        size = LANES + halves * LANES
        row = jnp.where(valid, row, -1)
        position = iota((size, LANES), 0)
        for n in range(16):
            hot = jnp.where(position == row[n : n + 1], 1.0, 0.0).astype(BF16)
            target_ref[g - 1, :, n * LANES : (n + 1) * LANES] = hot

    ready("basis")

    rates = decay_rates(basis)

    def radial_rows(weights, octet):
        dist8 = dist_ref[0, pl.ds(octet * 8, 8), :]
        weight8 = dist_ref[1, pl.ds(octet * 8, 8), :]
        slope8 = dist_ref[2, pl.ds(octet * 8, 8), :]
        values = jnp.concatenate([jnp.exp(-rates * dist8[j : j + 1]) for j in range(8)], axis=1)
        high, low = split_wide(values)
        stacked = jnp.concatenate([high, low, high, low], axis=0).astype(BF16)
        both = dot_tn(weights, stacked)
        rows = []
        for j in range(8):
            before = both[:hidden, j * LANES : (j + 1) * LANES]
            change = both[hidden:, j * LANES : (j + 1) * LANES]
            gate = sigmoid(before)
            after = before * gate
            gain = gate + after * (1.0 - gate)
            weight = weight8[j : j + 1]
            rows.append((weight * after, slope8[j : j + 1] * after + weight * (gain * change)))
        return rows

    def radial_one_step(octet, carry):
        for j, (value, slope) in enumerate(radial_rows(basis_ref[0], octet)):
            wh_ref[octet * 8 + j] = value
            slope_ref[octet * 8 + j] = slope
        return carry

    lax.fori_loop(0, groups * 2, radial_one_step, 0)

    def radial_two_step(octet, carry):
        rows = radial_rows(basis_ref[1], octet)
        lanes = pl.ds(pl.multiple_of(octet * 8 * LANES, 8 * LANES), 8 * LANES)
        for i in range(2):
            wh2_ref[i, :, lanes] = data_stack(jnp.concatenate([row[i] for row in rows], axis=1))
        return carry

    lax.fori_loop(0, 2, radial_two_step, 0)

    def moment_step(step, carry):
        g, part = step // (hidden // 16), step % (hidden // 16)
        lanes = pl.ds(pl.multiple_of(g * LANES, LANES), LANES)
        sums = [[[jnp.zeros((8, LANES), F32) for _ in range(4)] for _ in range(kinds)] for _ in range(2)]
        for n in range(16):
            e = g * 16 + n
            kind = kind_ref[e]
            masks = [kind == float(s) for s in range(kinds)]
            for i in range(2):
                value = wh_ref[e, pl.ds(pl.multiple_of(part * 16 + i * 8, 8), 8), :]
                parts = [value] + [value * r_ref[x, e] for x in range(3)]
                for s in range(kinds):
                    for j in range(4):
                        sums[i][s][j] = sums[i][s][j] + jnp.where(masks[s], parts[j], 0.0)
        for i in range(2):
            for s in range(kinds):
                place = pl.ds(pl.multiple_of(s * hidden + part * 16 + i * 8, 8), 8)
                for j in range(4):
                    moment_ref[j, place, lanes] = sums[i][s][j]
        return carry

    lax.fori_loop(0, groups * (hidden // 16), moment_step, 0)

    ready("slots", "mixes", "turns")

    scalar_one = dot_nn(slots_ref[0], data_stack(moment_ref[0]))
    vector_one = [dot_nn(slots_ref[1], data_stack(moment_ref[1 + x])) for x in range(3)]
    squares_one = sum(v * v for v in vector_one)
    before_one = dot_nn(
        mixes_ref[0], jnp.concatenate([data_stack(scalar_one), data_stack(squares_one)], axis=0)
    )
    gate_one = sigmoid(before_one)
    features = [before_one * gate_one] + [dot_nn(turns_ref[0], data_stack(v)) for v in vector_one]
    gain_one = gate_one * (1.0 + before_one * (1.0 - gate_one))
    for j in range(4):
        rows = slice(j * channels, (j + 1) * channels)
        feat_ref[rows, 0:atoms], feat_ref[rows, atoms : 2 * atoms] = split(features[j])
    node_ref[4, :, 0:atoms] = gain_one
    for x in range(3):
        node_ref[5 + x, :, 0:atoms] = vector_one[x]

    ready("high", "low", "paths")

    def edge_step(step, carry):
        lanes = pl.ds(pl.multiple_of(step * 256, 256), 256)
        source_ref[:, lanes] = dot_nn(feat_ref[...], pair_ref[:, lanes])
        for i in range(2):
            radial_ref[i, :, lanes] = dot_nn(paths_ref[...], wh2_ref[i, :, lanes])
        return carry

    lax.fori_loop(0, own_edges // 256, edge_step, 0)

    def sum_step(part, carry):
        def rows(j):
            return pl.ds(pl.multiple_of(j * channels + part * 8, 8), 8)

        sums = [jnp.zeros((8, LANES), F32) for _ in range(4)]
        for n in range(16):
            lanes = slice(n * LANES, (n + 1) * LANES)
            t = source_ref[rows(0), lanes]
            u = [source_ref[rows(1 + x), lanes] for x in range(3)]
            paths = [radial_ref[0, rows(j), lanes] for j in range(4)]
            r = [r_ref[x, n] for x in range(3)]
            along = r[0] * u[0] + r[1] * u[1] + r[2] * u[2]
            sums[0] = sums[0] + (paths[0] * t + paths[1] * along)
            turned = paths[2] * t
            for x in range(3):
                sums[1 + x] = sums[1 + x] + (turned * r[x] + paths[3] * u[x])
        for j in range(4):
            node_ref[j, pl.ds(pl.multiple_of(part * 8, 8), 8), 0:LANES] = sums[j]
        return carry

    lax.fori_loop(0, channels // 8, sum_step, 0)

    ready("readout", "pulls")

    scalar_two = node_ref[0, :, 0:LANES]
    vector_two = [node_ref[1 + x, :, 0:LANES] for x in range(3)]
    squares_two = sum(v * v for v in vector_two)
    before_two = dot_nn(
        mixes_ref[1], jnp.concatenate([data_stack(scalar_two), data_stack(squares_two)], axis=0)
    )
    gate_two = sigmoid(before_two)
    readout = readout_ref[...]
    energy_ref[0, 0] = jnp.sum(readout * (before_two * gate_two), axis=0, keepdims=True)
    dbefore_two = readout * (gate_two * (1.0 + before_two * (1.0 - gate_two)))
    dbefore_two = data_stack(dbefore_two)
    dscalar_two = dot_nn(turns_ref[4], dbefore_two)
    dsquares_two = dot_nn(turns_ref[5], dbefore_two)
    node_ref[0, :, 0:LANES] = dscalar_two
    for x in range(3):
        node_ref[1 + x, :, 0:LANES] = 2.0 * vector_two[x] * dsquares_two

    def back_step(n, carry):
        lanes = pl.ds(pl.multiple_of(n * LANES, LANES), LANES)
        r = [jnp.concatenate([r_ref[x, n]] * 2, axis=0) for x in range(3)]
        totals = [jnp.zeros((16, LANES), F32) for _ in range(4)]
        for part in range(channels // 16):

            def rows(j):
                return slice(j * channels + part * 16, j * channels + part * 16 + 16)

            t = source_ref[rows(0), lanes]
            u = [source_ref[rows(1 + x), lanes] for x in range(3)]
            paths = [radial_ref[0, rows(j), lanes] for j in range(4)]
            ds = node_ref[0, rows(0), 0:LANES]
            dv = [node_ref[1 + x, rows(0), 0:LANES] for x in range(3)]
            push = paths[1] * ds
            facing = r[0] * dv[0] + r[1] * dv[1] + r[2] * dv[2]
            along = r[0] * u[0] + r[1] * u[1] + r[2] * u[2]
            meeting = dv[0] * u[0] + dv[1] * u[1] + dv[2] * u[2]
            turned = paths[2] * t
            dsource = [paths[0] * ds + paths[2] * facing]
            for x in range(3):
                dsource.append(push * r[x] + paths[3] * dv[x])
                totals[x] = totals[x] + (push * u[x] + turned * dv[x])
            dradial = [ds * t, ds * along, t * facing, meeting]
            slopes = [radial_ref[1, rows(j), lanes] for j in range(4)]
            products = [dradial[j] * slopes[j] for j in range(4)]
            totals[3] = totals[3] + ((products[0] + products[1]) + (products[2] + products[3]))
            for j in range(4):
                dsource_ref[0, rows(j), lanes], dsource_ref[1, rows(j), lanes] = split(dsource[j])
        dd = 2.0 * jnp.sum(totals[3], axis=0, keepdims=True)
        for x in range(3):
            total = jnp.sum(totals[x], axis=0, keepdims=True)
            dr_ref[x : x + 1, lanes] = total + dd * r_ref[x, n, 0:1, :]
        return carry

    lax.fori_loop(0, 16, back_step, 0)

    source_ref[:, 0:atoms] = dot_nt(dsource_ref[0], pair_ref[0:atoms, :]) + dot_nt(
        dsource_ref[1], pair_ref[0:atoms, :]
    )
    dfeat = source_ref[:, 0:atoms]
    gain_one = node_ref[4, :, 0:atoms]
    vector_one = [node_ref[5 + x, :, 0:atoms] for x in range(3)]
    dbefore_one = data_stack(dfeat[0:channels] * gain_one)
    dscalar_one = dot_nn(turns_ref[2], dbefore_one)
    dsquares_one = dot_nn(turns_ref[3], dbefore_one)
    dmoment_ref[0] = dot_nn(pulls_ref[0], data_stack(dscalar_one))
    for x in range(3):
        du = data_stack(dfeat[(1 + x) * channels : (2 + x) * channels])
        dvector = 2.0 * vector_one[x] * dsquares_one + dot_nn(turns_ref[1], du)
        dmoment_ref[1 + x] = dot_nn(pulls_ref[1], data_stack(dvector))

    def one_back_step(step, carry):
        g = step // 4
        lanes = pl.ds(pl.multiple_of(g * LANES, LANES), LANES)
        edges = [step * 4 + j for j in range(4)]
        totals = [[jnp.zeros((8, LANES), F32) for _ in range(4)] for _ in range(4)]
        for part in range(hidden // 8):
            rows = slice(part * 8, part * 8 + 8)
            pulls = [
                [dmoment_ref[m, s * hidden + part * 8 : s * hidden + part * 8 + 8, lanes] for m in range(4)]
                for s in range(kinds)
            ]
            for j, e in enumerate(edges):
                kind = kind_ref[e]
                chosen = pulls[0]
                for s in range(1, kinds):
                    mask = kind == float(s)
                    chosen = [jnp.where(mask, pulls[s][m], chosen[m]) for m in range(4)]
                r = [r_ref[x, e] for x in range(3)]
                dwh = chosen[0] + r[0] * chosen[1] + r[1] * chosen[2] + r[2] * chosen[3]
                value = wh_ref[e, rows, :]
                totals[j][3] = totals[j][3] + dwh * slope_ref[e, rows, :]
                for x in range(3):
                    totals[j][x] = totals[j][x] + value * chosen[1 + x]
        for j, e in enumerate(edges):
            at = pl.ds(pl.multiple_of(e * LANES, LANES), LANES)
            dd = 2.0 * jnp.sum(totals[j][3], axis=0, keepdims=True)
            for x in range(3):
                change = jnp.sum(totals[j][x], axis=0, keepdims=True) + dd * r_ref[x, e, 0:1, :]
                dr_ref[4 + x : 5 + x, at] = change
        return carry

    lax.fori_loop(0, groups * 4, one_back_step, 0)

    pieces = []
    for e in range(groups * 16):
        at = slice(e * LANES, (e + 1) * LANES)
        piece = dr_ref[:, at]
        low = pltpu.roll(piece, 4, 0)
        if e < 16:
            piece = jnp.where((sub8 & 3) == 3, 0.0, piece + low)
        else:
            piece = jnp.where((sub8 & 3) == 3, 0.0, jnp.where(sub8 < 4, low, piece))
        pieces.append(piece)
    centres = [sum(pieces[g * 16 : g * 16 + 16]) for g in range(groups)]
    own_change = jnp.concatenate(pieces[:16], axis=1)
    own_high, own_low = split_wide(own_change)
    moved = dot_nt(jnp.concatenate([own_high, own_low], axis=0).astype(BF16), pair_ref[0:atoms, :])
    moved = moved[0:8] + moved[8:16]
    moved = [moved[:, g * LANES : (g + 1) * LANES] - centres[g] for g in range(groups)]

    sent_totals = [jnp.zeros((8, LANES), F32) for _ in range(halves)]
    inner = {}
    for g in range(1, groups):
        members = range((g - 1) * 8, min(g * 8, len(near)))
        change = jnp.concatenate(pieces[g * 16 : g * 16 + 16], axis=1)
        high, low = split_wide(change)
        owner = (iota(change.shape, 1) & (LANES - 1)) >> 4
        stack = [high, low]
        for q in members:
            here = owner == q % 8
            stack += [jnp.where(here, high, 0.0), jnp.where(here, low, 0.0)]
        spread = dot_nt(jnp.concatenate(stack, axis=0).astype(BF16), target_ref[g - 1])
        for h in range(halves):
            lanes = slice(LANES + h * LANES, 2 * LANES + h * LANES)
            sent_totals[h] = sent_totals[h] + (spread[0:8, lanes] + spread[8:16, lanes])
        for i, q in enumerate(members):
            at = 16 + i * 16
            inner[q] = spread[at : at + 8, 0:LANES] + spread[at + 8 : at + 16, 0:LANES]

    spot = lane8 & 15
    for w in range(windows):
        block = jnp.take_along_axis(sent_totals[w // 8], (w % 8) * 16 + spot, axis=1)
        grad_ref[w] = jnp.where(sub8 < 4, 0.0, block)
    grad_ref[own_place] = grad_ref[own_place] + jnp.where(sub8 < 4, moved[0], 0.0)
    for q in range(len(near)):
        block = jnp.take_along_axis(moved[1 + q // 8], (q % 8) * 16 + spot, axis=1)
        grad_ref[near_places[q]] = grad_ref[near_places[q]] + jnp.where(sub8 < 4, inner[q], block)


def send_along(value, axis, steps):
    count = lax.axis_size(axis)
    return lax.ppermute(value, axis, [(i, (i + steps) % count) for i in range(count)])


def axis_steps(count):
    return list(range(count)) if count <= REACH else list(range(-2, 3))


def per_device(
    positions,
    species,
    neighbours,
    send_list,
    embedding,
    radial_in,
    radial_out_one,
    radial_in_two,
    radial_out_two,
    mix_scalar_one,
    mix_square_one,
    mix_vector_one,
    mix_scalar_two,
    mix_square_two,
    readout,
):
    dims = tuple(lax.axis_size(axis) for axis in AXES)
    windows = 1
    for count in dims:
        windows *= window_size(count)
    whole = windows == dims[0] * dims[1] * dims[2] and windows <= 16
    near = [step for step in itertools.product(*[near_steps(n) for n in dims])][1:]
    groups = 1 + -(-len(near) // 8)
    halves = -(-windows * GHOSTS // LANES)
    atoms = groups * LANES
    hidden = radial_in.shape[1]
    kinds, channels = embedding.shape
    copies = windows if whole else 1
    smem = pl.BlockSpec(memory_space=pltpu.SMEM)
    vmem = pl.BlockSpec(memory_space=pltpu.VMEM)

    packed = pl.pallas_call(
        functools.partial(pack_kernel, copies),
        out_shape=jax.ShapeDtypeStruct((copies, 8, LANES), F32),
        in_specs=[smem, vmem, vmem, vmem],
        out_specs=vmem,
    )(send_list, positions, species, neighbours)

    if whole:
        table = lax.all_to_all(packed, AXES, 0, 0, tiled=True)
    else:
        table = packed.reshape(1, 1, 1, 8, LANES)
        for dim, axis in reversed(list(enumerate(AXES))):
            parts = [
                send_along(table, axis, -step) if step else table for step in axis_steps(dims[dim])
            ]
            table = jnp.concatenate(parts, axis=dim)
        table = table.reshape(windows, 8, LANES)

    weights = (
        embedding,
        radial_in,
        radial_out_one,
        radial_in_two,
        radial_out_two,
        mix_scalar_one,
        mix_square_one,
        mix_vector_one,
        mix_scalar_two,
        mix_square_two,
        readout.reshape(1, channels),
    )
    rows = groups * 16
    edges = 16 * LANES
    prepared = pl.pallas_call(
        functools.partial(prepare_kernel, dims),
        out_shape=(
            jax.ShapeDtypeStruct((atoms, edges), BF16),
            jax.ShapeDtypeStruct((2, 4 * radial_in.shape[0], 2 * hidden), BF16),
            jax.ShapeDtypeStruct((2, channels, 3 * kinds * hidden), BF16),
            jax.ShapeDtypeStruct((2, kinds * hidden, 3 * channels), BF16),
            jax.ShapeDtypeStruct((2, channels, 6 * channels), BF16),
            jax.ShapeDtypeStruct((6, channels, 3 * channels), BF16),
            jax.ShapeDtypeStruct((4 * channels, 3 * hidden), BF16),
            jax.ShapeDtypeStruct((channels, LANES), F32),
        ),
        in_specs=[vmem] * 12,
        out_specs=(vmem,) * 8,
        compiler_params=pltpu.CompilerParams(vmem_limit_bytes=VMEM_BYTES),
        cost_estimate=pl.CostEstimate(flops=0, bytes_accessed=8 * 1024 * 1024, transcendentals=0),
    )(neighbours, *weights)
    grads, energy = pl.pallas_call(
        functools.partial(main_kernel, dims, near, whole),
        out_shape=(
            jax.ShapeDtypeStruct((windows, 8, LANES), F32),
            jax.ShapeDtypeStruct((1, 1, 1, LANES), F32),
        ),
        in_specs=[vmem] * 2 + [pl.BlockSpec(memory_space=pltpu.HBM)] * len(prepared),
        out_specs=(vmem, vmem),
        scratch_shapes=[
            pltpu.VMEM((3, rows, 8, LANES), F32),
            pltpu.VMEM((rows, 8, LANES), F32),
            pltpu.VMEM((3, rows, LANES), F32),
            pltpu.VMEM((rows, hidden, LANES), F32),
            pltpu.VMEM((rows, hidden, LANES), F32),
            pltpu.VMEM((2, 3 * hidden, edges), BF16),
            pltpu.VMEM((4, kinds * hidden, atoms), F32),
            pltpu.VMEM((groups - 1, LANES + halves * LANES, edges), BF16),
            pltpu.VMEM((4 * channels, 2 * atoms), BF16),
            pltpu.VMEM((4 * channels, edges), F32),
            pltpu.VMEM((2, 4 * channels, edges), F32),
            pltpu.VMEM((8, channels, atoms), F32),
            pltpu.VMEM((2, 4 * channels, edges), BF16),
            pltpu.VMEM((8, rows * LANES), F32),
            pltpu.VMEM((4, kinds * hidden, atoms), F32),
            pltpu.VMEM((2 * atoms, edges), BF16),
        ]
        + [pltpu.VMEM(p.shape, p.dtype) for p in prepared[1:]]
        + [pltpu.SemaphoreType.DMA((len(prepared) + 1,))],
        compiler_params=pltpu.CompilerParams(vmem_limit_bytes=VMEM_BYTES),
    )(table, neighbours, *prepared)

    if whole:
        returned = lax.all_to_all(grads, AXES, 0, 0, tiled=True)
    else:
        returned = grads.reshape(tuple(window_size(n) for n in dims) + (8, LANES))
        for dim, axis in enumerate(AXES):
            total = None
            for place, step in enumerate(axis_steps(dims[dim])):
                part = lax.slice_in_dim(returned, place, place + 1, axis=dim)
                part = send_along(part, axis, step) if step else part
                total = part if total is None else total + part
            returned = total
        returned = returned.reshape(1, 8, LANES)

    forces = pl.pallas_call(
        functools.partial(forces_kernel, copies),
        out_shape=jax.ShapeDtypeStruct((3, 1, 1, 1, LANES), F32),
        in_specs=[smem, vmem],
        out_specs=vmem,
    )(send_list, returned)
    return (forces.reshape(3, 1, 1, 1, LANES), energy)


def solution(mesh):
    spread = ("groups", "gx")
    return jax.shard_map(
        per_device,
        mesh=mesh,
        in_specs=(
            P(None, spread, "gy", "gz", None),
            P(spread, "gy", "gz", None),
            P(spread, "gy", "gz", None, None),
            P(spread, "gy", "gz", None),
        )
        + (P(),) * 11,
        out_specs=(P(None, spread, "gy", "gz", None), P(spread, "gy", "gz", None)),
        check_vma=False,
    )
```

```python
import functools
import itertools

import jax
import jax.numpy as jnp
from jax import lax
from jax.experimental import pallas as pl
from jax.experimental.pallas import tpu as pltpu
from jax.sharding import PartitionSpec as P

MESSAGE_SCALE = 0.125
CUTOFF_SQUARED = 16.0
AXES = ("gx", "gy", "gz")
LANES = 128
GHOSTS = 16
REACH = 5
VMEM_BYTES = 60 * 1024 * 1024
MAIN_BYTES = 55040 * 1024
F32 = jnp.float32
BF16 = jnp.bfloat16


def window_size(count):
    return min(count, REACH)


def window_place(relative, base, count):
    if count > REACH:
        return relative + 2
    place = relative + base
    for _ in range(2):
        place = jnp.where(place < 0, place + count, place)
    for _ in range(2):
        place = jnp.where(place >= count, place - count, place)
    return place


def near_steps(count):
    return [0, 1, -1][: min(count, 3)]


def near_place(step, count):
    if count >= 3:
        return jnp.where(step < 0, step + 3, step)
    return jnp.where(step == 0, 0, 1)


def split(x):
    high = x.astype(BF16)
    return high, (x - high.astype(F32)).astype(BF16)


def split_wide(x):
    high = x.astype(BF16).astype(F32)
    return high, x - high


def weight_stack(w):
    high, low = split(w)
    return jnp.concatenate([high, low, high], axis=0)


def data_stack(x):
    high, low = split(x)
    return jnp.concatenate([high, high, low], axis=0)


def dot_nn(a, b):
    return lax.dot_general(a, b, (((1,), (0,)), ((), ())), preferred_element_type=F32)


def dot_tn(a, b):
    return lax.dot_general(a, b, (((0,), (0,)), ((), ())), preferred_element_type=F32)


def dot_nt(a, b):
    return lax.dot_general(a, b, (((1,), (1,)), ((), ())), preferred_element_type=F32)


def product_nn(w_high, w_low, x):
    high, low = split(x)
    return dot_nn(w_high, high) + dot_nn(w_low, high) + dot_nn(w_high, low)


def sigmoid(v):
    return 0.5 + 0.5 * jnp.tanh(0.5 * v)


def pick_lanes(row, index):
    return jnp.take_along_axis(jnp.broadcast_to(row, index.shape), index, axis=1)


def iota(shape, dim):
    return lax.broadcasted_iota(jnp.int32, shape, dim)


def pack_kernel(copies, send_ref, pos_ref, species_ref, neigh_ref, out_ref):
    lane = iota((8, LANES), 1)
    row = iota((8, LANES), 0)
    sent = jnp.zeros((8, LANES), jnp.int32)
    for s in range(GHOSTS):
        sent = jnp.where((lane & (GHOSTS - 1)) == s, send_ref[0, 0, 0, s], sent)
    block = jnp.zeros((8, LANES), F32)
    for x in range(3):
        block = jnp.where(row == x, pos_ref[x, 0, 0], block)
    block = jnp.where(row == 3, species_ref[0, 0].astype(F32), block)
    neigh = neigh_ref[0, 0, 0]
    for half in range(2):
        lists = jnp.take_along_axis(neigh[half * 8 : half * 8 + 8], sent, axis=1).astype(F32)
        kept = jnp.where((lane >> 4) == row, lists, 0.0)
        block = jnp.where(row == 4 + half, jnp.sum(kept, axis=0, keepdims=True), block)
    block = jnp.where(row == 6, sent.astype(F32), block)
    for w in range(copies):
        out_ref[w] = block


def forces_kernel(count, send_ref, parts_ref, out_ref):
    total = parts_ref[0]
    for w in range(1, count):
        total = total + parts_ref[w]
    lane = iota((8, LANES), 1)
    slot = jnp.full((8, LANES), -1, jnp.int32)
    for s in range(GHOSTS):
        slot = jnp.where(lane == send_ref[0, 0, 0, s], s, slot)
    moved = jnp.take_along_axis(total, jnp.maximum(slot, 0), axis=1)
    moved = jnp.where(slot >= 0, moved, 0.0)
    for x in range(3):
        out_ref[x, 0, 0] = -(total[x : x + 1] + moved[4 + x : 5 + x])


def decay_rates(basis):
    rates = jnp.zeros((basis, LANES), F32)
    row = iota((basis, LANES), 0)
    for m in range(basis):
        rates = jnp.where(row == m, 0.08 * 2.0 ** (m / 2.0), rates)
    return rates


def ghost_parts(named):
    ghost = jnp.maximum(named - LANES, 0)
    block_id, slot = ghost >> 4, ghost & 15
    first = (block_id * 57) >> 9
    rest = block_id - first * 9
    second = (rest * 11) >> 5
    return [first - 1, second - 1, rest - second * 3 - 1], slot


def wide_stack(w):
    high, low = split(w)
    return jnp.concatenate([high, low, high], axis=1)


def turned_stack(w):
    return wide_stack(jnp.transpose(w))


def prepare_kernel(
    dims,
    neigh_ref,
    embedding_ref,
    win_one_ref,
    wout_one_ref,
    win_two_ref,
    wout_two_ref,
    mss_one_ref,
    msq_one_ref,
    mv_one_ref,
    mss_two_ref,
    msq_two_ref,
    readout_ref,
    pair_ref,
    slots_ref,
    pulls_ref,
    mixes_ref,
    turns_ref,
    paths_ref,
):
    atoms = pair_ref.shape[0]
    basis, hidden = win_one_ref.shape
    kinds, channels = embedding_ref.shape
    near_sizes = [len(near_steps(n)) for n in dims]
    entries = neigh_ref[0, 0, 0]
    named = jnp.maximum(entries, 0)
    shift, slot = ghost_parts(named)
    steps = [near_place(shift[a], dims[a]) for a in range(3)]
    order = (steps[0] * near_sizes[1] + steps[1]) * near_sizes[2] + steps[2]
    row = jnp.where(named < LANES, named, LANES + (order - 1) * GHOSTS + slot)
    row = jnp.where(entries >= 0, row, -1)
    position = iota((atoms, LANES), 0)
    for n in range(16):
        hot = jnp.where(position == row[n : n + 1], 1.0, 0.0).astype(BF16)
        pair_ref[:, n * LANES : (n + 1) * LANES] = hot

    rates = decay_rates(basis)
    for i, win_ref in enumerate((win_one_ref, win_two_ref)):
        win = win_ref[...]
        both = jnp.concatenate([win, -rates[:, :hidden] * win], axis=1)
        high, low = split_wide(both)
        stack = jnp.concatenate([high, high, low, low], axis=0).astype(BF16)
        turns_ref[6, i * 4 * basis : (i + 1) * 4 * basis, 0 : 2 * hidden] = stack
    for j in range(2):
        columns = wout_one_ref[:, j * channels : (j + 1) * channels]
        rows = [columns * embedding_ref[s : s + 1, :] for s in range(kinds)]
        combined = jnp.concatenate(rows, axis=0)
        high, low = split_wide(combined)
        slots_ref[j] = jnp.transpose(jnp.concatenate([high, low, high], axis=0)).astype(BF16)
        pulls_ref[j] = wide_stack(combined)
    pairs = ((mss_one_ref, msq_one_ref), (mss_two_ref, msq_two_ref))
    for i, (scalar_ref, square_ref) in enumerate(pairs):
        mixes_ref[i] = jnp.concatenate(
            [turned_stack(scalar_ref[...]), turned_stack(square_ref[...])], axis=1
        )
        turns_ref[2 + 2 * i] = wide_stack(scalar_ref[...])
        turns_ref[3 + 2 * i] = wide_stack(square_ref[...])
    turns_ref[0] = turned_stack(mv_one_ref[...])
    turns_ref[1] = wide_stack(mv_one_ref[...])
    high, low = split_wide(wout_two_ref[...])
    paths_ref[...] = jnp.transpose(jnp.concatenate([high, low, high], axis=0)).astype(BF16)
    read = jnp.transpose(jnp.broadcast_to(readout_ref[...], (LANES, channels)))
    turns_ref[6, :, LANES : 2 * LANES], turns_ref[6, :, 2 * LANES : 3 * LANES] = split(read)
    turns_ref[6, 8 * basis : channels, 0:LANES] = jnp.zeros((channels - 8 * basis, LANES), BF16)


def main_kernel(
    dims,
    near,
    whole,
    rank,
    table_ref,
    neigh_ref,
    pair_hbm,
    slots_hbm,
    pulls_hbm,
    mixes_hbm,
    turns_hbm,
    paths_hbm,
    grad_ref,
    energy_ref,
    r_ref,
    kind_ref,
    dist_ref,
    wh_ref,
    slope_ref,
    wh2_ref,
    moment_ref,
    target_ref,
    feat_ref,
    source_ref,
    radial_ref,
    node_ref,
    dsource_ref,
    dr_ref,
    dmoment_ref,
    pair_ref,
    slots_ref,
    pulls_ref,
    mixes_ref,
    turns_ref,
    paths_ref,
    copy_sem,
    place_ref,
    dfeat_ref,
):
    atoms = pair_hbm.shape[0]
    moves = {}
    for i, (name, source, target) in enumerate(
        (
            ("turns", turns_hbm, turns_ref),
            ("slots", slots_hbm, slots_ref),
            ("mixes", mixes_hbm, mixes_ref),
            ("high", pair_hbm, pair_ref.at[0:atoms]),
            ("low", pair_hbm, pair_ref.at[atoms : 2 * atoms]),
            ("paths", paths_hbm, paths_ref),
            ("pulls", pulls_hbm, pulls_ref),
        )
    ):
        moves[name] = pltpu.make_async_copy(source, target, copy_sem.at[i])
        moves[name].start()

    def ready(*names):
        for name in names:
            moves.pop(name).wait()

    wsize = tuple(window_size(n) for n in dims)
    windows = wsize[0] * wsize[1] * wsize[2]
    halves = -(-windows * GHOSTS // LANES)
    groups = 1 + -(-len(near) // 8)
    channels = LANES
    hidden = paths_ref.shape[1] // 3
    kinds = pulls_ref.shape[1] // hidden
    basis = rank
    own_edges = 16 * LANES

    lane16 = iota((16, LANES), 1)
    sub16 = iota((16, LANES), 0)
    lane8 = iota((8, LANES), 1)
    sub8 = iota((8, LANES), 0)
    bases = [lax.axis_index(axis) if whole else 0 for axis in AXES]
    near_sizes = [len(near_steps(n)) for n in dims]

    def flat(steps):
        places = [window_place(steps[a], bases[a], dims[a]) for a in range(3)]
        return (places[0] * wsize[1] + places[1]) * wsize[2] + places[2]

    own_place = flat((0, 0, 0))
    near_places = [flat(step) for step in near]

    sent = [jnp.zeros((8, LANES), F32) for _ in range(halves)]
    for w in range(windows):
        block = table_ref[w]
        index = jnp.broadcast_to(block[6:7], (8, LANES)).astype(jnp.int32)
        picked = jnp.take_along_axis(block, index, axis=1)
        sent[w // 8] = jnp.where((lane8 >> 4) == w % 8, picked, sent[w // 8])

    for g in range(groups):
        members = [] if g == 0 else list(range((g - 1) * 8, min(g * 8, len(near))))
        if g == 0:
            entries = neigh_ref[0, 0, 0]
            own_block = table_ref[own_place]
            centre = [own_block[x : x + 1] for x in range(3)]
            steps = [0, 0, 0]
        else:
            centre8 = jnp.zeros((8, LANES), F32)
            listed = [jnp.full((8, LANES), -1.0, F32) for _ in range(2)]
            steps = [jnp.zeros((16, LANES), jnp.int32) for _ in range(3)]
            for q in members:
                block = table_ref[near_places[q]]
                here = (lane8 >> 4) == q % 8
                index = jnp.broadcast_to(block[6:7], (8, LANES)).astype(jnp.int32)
                centre8 = jnp.where(here, jnp.take_along_axis(block, index, axis=1), centre8)
                for half in range(2):
                    rows = pick_lanes(block[4 + half : 5 + half], sub8 * 16 + (lane8 & 15))
                    listed[half] = jnp.where(here, rows, listed[half])
                for a in range(3):
                    if near[q][a]:
                        steps[a] = jnp.where((lane16 >> 4) == q % 8, near[q][a], steps[a])
            entries = jnp.concatenate(listed, axis=0).astype(jnp.int32)
            centre = [centre8[x : x + 1] for x in range(3)]
        valid = entries >= 0
        named = jnp.maximum(entries, 0)
        local = named < LANES
        local_index = jnp.where(local, named, 0)
        shift, slot = ghost_parts(named)
        sent_index = flat([shift[a] + steps[a] for a in range(3)]) * GHOSTS + slot
        values = []
        for x in range(4):
            if g == 0:
                inside = pick_lanes(own_block[x : x + 1], local_index)
            else:
                inside = jnp.zeros((16, LANES), F32)
                for q in members:
                    rows = pick_lanes(table_ref[near_places[q], x : x + 1, :], local_index)
                    inside = jnp.where((lane16 >> 4) == q % 8, rows, inside)
            outside = jnp.zeros((16, LANES), F32)
            for h in range(halves):
                rows = pick_lanes(sent[h][x : x + 1], sent_index & (LANES - 1))
                outside = jnp.where((sent_index >> 7) == h, rows, outside)
            if x < 3:
                outside = outside + shift[x].astype(F32)
            values.append(jnp.where(local, inside, outside))
        relative = [values[x] - centre[x] for x in range(3)]
        square = relative[0] * relative[0] + relative[1] * relative[1] + relative[2] * relative[2]
        linear = 1.0 - square / CUTOFF_SQUARED
        scale = jnp.where(valid, MESSAGE_SCALE, 0.0)
        dist_ref[0, g * 16 : g * 16 + 16, :] = square
        dist_ref[1, g * 16 : g * 16 + 16, :] = linear * linear * scale
        dist_ref[2, g * 16 : g * 16 + 16, :] = linear * scale * (-2.0 / CUTOFF_SQUARED)
        for n in range(16):
            for x in range(3):
                r_ref[x, g * 16 + n] = jnp.broadcast_to(relative[x][n : n + 1], (8, LANES))
            kind_ref[g * 16 + n] = jnp.broadcast_to(values[3][n : n + 1], (8, LANES))
        if g == 0:
            continue
        row = jnp.where(local, local_index, LANES + sent_index)
        place_ref[g - 1] = jnp.where(valid, row, -1)

    ready("turns")

    rates = decay_rates(basis)

    def radial_rows(weights, octet):
        dist8 = dist_ref[0, octet * 8 : octet * 8 + 8, :]
        weight8 = dist_ref[1, octet * 8 : octet * 8 + 8, :]
        slope8 = dist_ref[2, octet * 8 : octet * 8 + 8, :]
        values = jnp.concatenate([jnp.exp(-rates * dist8[j : j + 1]) for j in range(8)], axis=1)
        high, low = split_wide(values)
        stacked = jnp.concatenate([high, low, high, low], axis=0).astype(BF16)
        both = dot_tn(weights, stacked)
        rows = []
        for j in range(8):
            before = both[:hidden, j * LANES : (j + 1) * LANES]
            change = both[hidden:, j * LANES : (j + 1) * LANES]
            gate = sigmoid(before)
            after = before * gate
            gain = gate + after * (1.0 - gate)
            weight = weight8[j : j + 1]
            rows.append((weight * after, slope8[j : j + 1] * after + weight * (gain * change)))
        return rows

    def radial_one_step(octet, carry):
        for j, (value, slope) in enumerate(radial_rows(turns_ref[6, 0 : 4 * basis, 0 : 2 * hidden], octet)):
            wh_ref[octet * 8 + j] = value
            slope_ref[octet * 8 + j] = slope
        return carry

    for octet in range(groups * 2):
        radial_one_step(octet, 0)

    def radial_two_step(octet, carry):
        rows = radial_rows(turns_ref[6, 4 * basis : 8 * basis, 0 : 2 * hidden], octet)
        lanes = slice(octet * 8 * LANES, (octet + 1) * 8 * LANES)
        for i in range(2):
            wh2_ref[i, :, lanes] = data_stack(jnp.concatenate([row[i] for row in rows], axis=1))
        return carry

    for octet in range(2):
        radial_two_step(octet, 0)

    def moment_step(step, carry):
        g, part = step // (hidden // 16), step % (hidden // 16)
        lanes = pl.ds(pl.multiple_of(g * LANES, LANES), LANES)
        sums = [[[jnp.zeros((8, LANES), F32) for _ in range(4)] for _ in range(kinds)] for _ in range(2)]
        for n in range(16):
            e = g * 16 + n
            kind = kind_ref[e]
            masks = [kind == float(s) for s in range(kinds)]
            for i in range(2):
                value = wh_ref[e, pl.ds(pl.multiple_of(part * 16 + i * 8, 8), 8), :]
                parts = [value] + [value * r_ref[x, e] for x in range(3)]
                for s in range(kinds):
                    for j in range(4):
                        sums[i][s][j] = sums[i][s][j] + jnp.where(masks[s], parts[j], 0.0)
        for i in range(2):
            for s in range(kinds):
                place = pl.ds(pl.multiple_of(s * hidden + part * 16 + i * 8, 8), 8)
                for j in range(4):
                    moment_ref[j, place, lanes] = sums[i][s][j]
        return carry

    lax.fori_loop(0, groups * (hidden // 16), moment_step, 0)

    ready("slots", "mixes")

    scalar_one = dot_nn(slots_ref[0], data_stack(moment_ref[0]))
    vector_one = [dot_nn(slots_ref[1], data_stack(moment_ref[1 + x])) for x in range(3)]
    squares_one = sum(v * v for v in vector_one)
    before_one = dot_nn(
        mixes_ref[0], jnp.concatenate([data_stack(scalar_one), data_stack(squares_one)], axis=0)
    )
    gate_one = sigmoid(before_one)
    features = [before_one * gate_one] + [dot_nn(turns_ref[0], data_stack(v)) for v in vector_one]
    gain_one = gate_one * (1.0 + before_one * (1.0 - gate_one))
    for j in range(4):
        rows = slice(j * channels, (j + 1) * channels)
        feat_ref[rows, 0:atoms], feat_ref[rows, atoms : 2 * atoms] = split(features[j])
    node_ref[4, :, 0:atoms] = gain_one
    for x in range(3):
        node_ref[5 + x, :, 0:atoms] = vector_one[x]

    ready("high", "low", "paths")

    def edge_step(step, carry):
        lanes = slice(step * 256, step * 256 + 256)
        source_ref[:, lanes] = dot_nn(feat_ref[...], pair_ref[:, lanes])
        for i in range(2):
            radial_ref[i, :, lanes] = dot_nn(paths_ref[...], wh2_ref[i, :, lanes])
        position = iota((LANES + halves * LANES, LANES), 0)
        for i in range(2):
            n = step * 2 + i
            at = slice(n * LANES, n * LANES + LANES)
            for g in range(groups - 1):
                hot = position == place_ref[g, n : n + 1, :]
                target_ref[g, :, at] = jnp.where(hot, 1.0, 0.0).astype(BF16)
        return carry

    def sum_slots(step):
        for part in range(channels // 8):

            def rows(j):
                return slice(j * channels + part * 8, j * channels + part * 8 + 8)

            sums = [node_ref[j, rows(0), 0:LANES] if step else 0.0 for j in range(4)]
            for n in (2 * step, 2 * step + 1):
                lanes = slice(n * LANES, (n + 1) * LANES)
                t = source_ref[rows(0), lanes]
                u = [source_ref[rows(1 + x), lanes] for x in range(3)]
                paths = [radial_ref[0, rows(j), lanes] for j in range(4)]
                r = [r_ref[x, n] for x in range(3)]
                along = r[0] * u[0] + r[1] * u[1] + r[2] * u[2]
                sums[0] = sums[0] + (paths[0] * t + paths[1] * along)
                turned = paths[2] * t
                for x in range(3):
                    sums[1 + x] = sums[1 + x] + (turned * r[x] + paths[3] * u[x])
            for j in range(4):
                node_ref[j, rows(0), 0:LANES] = sums[j]

    for step in range(own_edges // 256):
        edge_step(step, 0)
        if step:
            sum_slots(step - 1)
    sum_slots(own_edges // 256 - 1)


    ready("pulls")

    scalar_two = node_ref[0, :, 0:LANES]
    vector_two = [node_ref[1 + x, :, 0:LANES] for x in range(3)]
    squares_two = sum(v * v for v in vector_two)
    before_two = dot_nn(
        mixes_ref[1], jnp.concatenate([data_stack(scalar_two), data_stack(squares_two)], axis=0)
    )
    gate_two = sigmoid(before_two)
    readout = sum(turns_ref[6, :, i * LANES : (i + 1) * LANES].astype(F32) for i in (1, 2))
    energy_ref[0, 0] = jnp.sum(readout * (before_two * gate_two), axis=0, keepdims=True)
    dbefore_two = readout * (gate_two * (1.0 + before_two * (1.0 - gate_two)))
    dbefore_two = data_stack(dbefore_two)
    dscalar_two = dot_nn(turns_ref[4], dbefore_two)
    dsquares_two = dot_nn(turns_ref[5], dbefore_two)
    node_ref[0, :, 0:LANES] = dscalar_two
    for x in range(3):
        node_ref[1 + x, :, 0:LANES] = 2.0 * vector_two[x] * dsquares_two

    def back_slot(n, half):
        lanes = slice(n * LANES, (n + 1) * LANES)
        r = [jnp.concatenate([r_ref[x, n]] * 2, axis=0) for x in range(3)]
        totals = [jnp.zeros((16, LANES), F32) for _ in range(4)]
        for part in range(half * channels // 32, (half + 1) * channels // 32):

            def rows(j):
                return slice(j * channels + part * 16, j * channels + part * 16 + 16)

            t = source_ref[rows(0), lanes]
            u = [source_ref[rows(1 + x), lanes] for x in range(3)]
            paths = [radial_ref[0, rows(j), lanes] for j in range(4)]
            ds = node_ref[0, rows(0), 0:LANES]
            dv = [node_ref[1 + x, rows(0), 0:LANES] for x in range(3)]
            push = paths[1] * ds
            facing = r[0] * dv[0] + r[1] * dv[1] + r[2] * dv[2]
            along = r[0] * u[0] + r[1] * u[1] + r[2] * u[2]
            meeting = dv[0] * u[0] + dv[1] * u[1] + dv[2] * u[2]
            turned = paths[2] * t
            dsource = [paths[0] * ds + paths[2] * facing]
            for x in range(3):
                dsource.append(push * r[x] + paths[3] * dv[x])
                totals[x] = totals[x] + (push * u[x] + turned * dv[x])
            dradial = [ds * t, ds * along, t * facing, meeting]
            slopes = [radial_ref[1, rows(j), lanes] for j in range(4)]
            products = [dradial[j] * slopes[j] for j in range(4)]
            totals[3] = totals[3] + ((products[0] + products[1]) + (products[2] + products[3]))
            for j in range(4):
                dsource_ref[0, rows(j), lanes], dsource_ref[1, rows(j), lanes] = split(dsource[j])
        dd = 2.0 * jnp.sum(totals[3], axis=0, keepdims=True)
        for x in range(3):
            total = jnp.sum(totals[x], axis=0, keepdims=True) + dd * r_ref[x, n, 0:1, :]
            if half:
                total = total + dr_ref[x : x + 1, lanes]
            dr_ref[x : x + 1, lanes] = total

    for half in range(2):
        for n in range(16):
            back_slot(n, half)
        size = channels // 2
        picked = [slice(j * channels + half * size, j * channels + half * size + size) for j in range(4)]
        stack = [dsource_ref[i, at, :] for i in range(2) for at in picked]
        spread = dot_nt(jnp.concatenate(stack, axis=0), pair_ref[0:atoms, :])
        for j in range(4):
            high = spread[j * size : (j + 1) * size]
            dfeat_ref[picked[j], :] = high + spread[(4 + j) * size : (5 + j) * size]

    dfeat = dfeat_ref[...]
    gain_one = node_ref[4, :, 0:atoms]
    vector_one = [node_ref[5 + x, :, 0:atoms] for x in range(3)]
    dbefore_one = data_stack(dfeat[0:channels] * gain_one)
    dscalar_one = dot_nn(turns_ref[2], dbefore_one)
    dsquares_one = dot_nn(turns_ref[3], dbefore_one)
    dmoment_ref[0] = dot_nn(pulls_ref[0], data_stack(dscalar_one))
    for x in range(3):
        du = data_stack(dfeat[(1 + x) * channels : (2 + x) * channels])
        dvector = 2.0 * vector_one[x] * dsquares_one + dot_nn(turns_ref[1], du)
        dmoment_ref[1 + x] = dot_nn(pulls_ref[1], data_stack(dvector))

    def one_back_step(step, carry):
        g = step // 4
        lanes = pl.ds(pl.multiple_of(g * LANES, LANES), LANES)
        edges = [step * 4 + j for j in range(4)]
        totals = [[jnp.zeros((8, LANES), F32) for _ in range(4)] for _ in range(4)]
        for part in range(hidden // 8):
            rows = slice(part * 8, part * 8 + 8)
            pulls = [
                [dmoment_ref[m, s * hidden + part * 8 : s * hidden + part * 8 + 8, lanes] for m in range(4)]
                for s in range(kinds)
            ]
            for j, e in enumerate(edges):
                kind = kind_ref[e]
                chosen = pulls[0]
                for s in range(1, kinds):
                    mask = kind == float(s)
                    chosen = [jnp.where(mask, pulls[s][m], chosen[m]) for m in range(4)]
                r = [r_ref[x, e] for x in range(3)]
                dwh = chosen[0] + r[0] * chosen[1] + r[1] * chosen[2] + r[2] * chosen[3]
                value = wh_ref[e, rows, :]
                totals[j][3] = totals[j][3] + dwh * slope_ref[e, rows, :]
                for x in range(3):
                    totals[j][x] = totals[j][x] + value * chosen[1 + x]
        for j, e in enumerate(edges):
            at = pl.ds(pl.multiple_of(e * LANES, LANES), LANES)
            dd = 2.0 * jnp.sum(totals[j][3], axis=0, keepdims=True)
            for x in range(3):
                change = jnp.sum(totals[j][x], axis=0, keepdims=True) + dd * r_ref[x, e, 0:1, :]
                dr_ref[4 + x : 5 + x, at] = change
        return carry

    lax.fori_loop(0, groups * 4, one_back_step, 0)

    pieces = []
    for e in range(groups * 16):
        at = slice(e * LANES, (e + 1) * LANES)
        piece = dr_ref[:, at]
        low = pltpu.roll(piece, 4, 0)
        if e < 16:
            piece = jnp.where((sub8 & 3) == 3, 0.0, piece + low)
        else:
            piece = jnp.where((sub8 & 3) == 3, 0.0, jnp.where(sub8 < 4, low, piece))
        pieces.append(piece)
    centres = [sum(pieces[g * 16 : g * 16 + 16]) for g in range(groups)]
    own_change = jnp.concatenate(pieces[:16], axis=1)
    own_high, own_low = split_wide(own_change)
    moved = dot_nt(jnp.concatenate([own_high, own_low], axis=0).astype(BF16), pair_ref[0:atoms, :])
    moved = moved[0:8] + moved[8:16]
    moved = [moved[:, g * LANES : (g + 1) * LANES] - centres[g] for g in range(groups)]

    sent_totals = [jnp.zeros((8, LANES), F32) for _ in range(halves)]
    inner = {}
    for g in range(1, groups):
        members = range((g - 1) * 8, min(g * 8, len(near)))
        change = jnp.concatenate(pieces[g * 16 : g * 16 + 16], axis=1)
        high, low = split_wide(change)
        owner = (iota(change.shape, 1) & (LANES - 1)) >> 4
        stack = [high, low]
        for q in members:
            here = owner == q % 8
            stack += [jnp.where(here, high, 0.0), jnp.where(here, low, 0.0)]
        spread = dot_nt(jnp.concatenate(stack, axis=0).astype(BF16), target_ref[g - 1])
        for h in range(halves):
            lanes = slice(LANES + h * LANES, 2 * LANES + h * LANES)
            sent_totals[h] = sent_totals[h] + (spread[0:8, lanes] + spread[8:16, lanes])
        for i, q in enumerate(members):
            at = 16 + i * 16
            inner[q] = spread[at : at + 8, 0:LANES] + spread[at + 8 : at + 16, 0:LANES]

    spot = lane8 & 15
    for w in range(windows):
        block = jnp.take_along_axis(sent_totals[w // 8], (w % 8) * 16 + spot, axis=1)
        grad_ref[w] = jnp.where(sub8 < 4, 0.0, block)
    grad_ref[own_place] = grad_ref[own_place] + jnp.where(sub8 < 4, moved[0], 0.0)
    for q in range(len(near)):
        block = jnp.take_along_axis(moved[1 + q // 8], (q % 8) * 16 + spot, axis=1)
        grad_ref[near_places[q]] = grad_ref[near_places[q]] + jnp.where(sub8 < 4, inner[q], block)


def send_along(value, axis, steps):
    count = lax.axis_size(axis)
    return lax.ppermute(value, axis, [(i, (i + steps) % count) for i in range(count)])


def axis_steps(count):
    return list(range(count)) if count <= REACH else list(range(-2, 3))


def per_device(
    positions,
    species,
    neighbours,
    send_list,
    embedding,
    radial_in,
    radial_out_one,
    radial_in_two,
    radial_out_two,
    mix_scalar_one,
    mix_square_one,
    mix_vector_one,
    mix_scalar_two,
    mix_square_two,
    readout,
):
    dims = tuple(lax.axis_size(axis) for axis in AXES)
    windows = 1
    for count in dims:
        windows *= window_size(count)
    whole = windows == dims[0] * dims[1] * dims[2] and windows <= 16
    near = [step for step in itertools.product(*[near_steps(n) for n in dims])][1:]
    groups = 1 + -(-len(near) // 8)
    halves = -(-windows * GHOSTS // LANES)
    atoms = groups * LANES
    hidden = radial_in.shape[1]
    kinds, channels = embedding.shape
    copies = windows if whole else 1
    smem = pl.BlockSpec(memory_space=pltpu.SMEM)
    vmem = pl.BlockSpec(memory_space=pltpu.VMEM)

    packed = pl.pallas_call(
        functools.partial(pack_kernel, copies),
        out_shape=jax.ShapeDtypeStruct((copies, 8, LANES), F32),
        in_specs=[smem, vmem, vmem, vmem],
        out_specs=vmem,
    )(send_list, positions, species, neighbours)

    if whole:
        table = lax.all_to_all(packed, AXES, 0, 0, tiled=True)
    else:
        table = packed.reshape(1, 1, 1, 8, LANES)
        for dim, axis in reversed(list(enumerate(AXES))):
            parts = [
                send_along(table, axis, -step) if step else table for step in axis_steps(dims[dim])
            ]
            table = jnp.concatenate(parts, axis=dim)
        table = table.reshape(windows, 8, LANES)

    weights = (
        embedding,
        radial_in,
        radial_out_one,
        radial_in_two,
        radial_out_two,
        mix_scalar_one,
        mix_square_one,
        mix_vector_one,
        mix_scalar_two,
        mix_square_two,
        readout.reshape(1, channels),
    )
    rows = groups * 16
    edges = 16 * LANES
    prepared = pl.pallas_call(
        functools.partial(prepare_kernel, dims),
        out_shape=(
            jax.ShapeDtypeStruct((atoms, edges), BF16),
            jax.ShapeDtypeStruct((2, channels, 3 * kinds * hidden), BF16),
            jax.ShapeDtypeStruct((2, kinds * hidden, 3 * channels), BF16),
            jax.ShapeDtypeStruct((2, channels, 6 * channels), BF16),
            jax.ShapeDtypeStruct((7, channels, 3 * channels), BF16),
            jax.ShapeDtypeStruct((4 * channels, 3 * hidden), BF16),
        ),
        in_specs=[vmem] * 12,
        out_specs=(vmem,) * 6,
        compiler_params=pltpu.CompilerParams(vmem_limit_bytes=VMEM_BYTES),
        cost_estimate=pl.CostEstimate(flops=0, bytes_accessed=8 * 1024 * 1024, transcendentals=0),
    )(neighbours, *weights)
    grads, energy = pl.pallas_call(
        functools.partial(main_kernel, dims, near, whole, radial_in.shape[0]),
        out_shape=(
            jax.ShapeDtypeStruct((windows, 8, LANES), F32),
            jax.ShapeDtypeStruct((1, 1, 1, LANES), F32),
        ),
        in_specs=[vmem] * 2 + [pl.BlockSpec(memory_space=pltpu.HBM)] * len(prepared),
        out_specs=(vmem, vmem),
        scratch_shapes=[
            pltpu.VMEM((3, rows, 8, LANES), F32),
            pltpu.VMEM((rows, 8, LANES), F32),
            pltpu.VMEM((3, rows, LANES), F32),
            pltpu.VMEM((rows, hidden, LANES), F32),
            pltpu.VMEM((rows, hidden, LANES), F32),
            pltpu.VMEM((2, 3 * hidden, edges), BF16),
            pltpu.VMEM((4, kinds * hidden, atoms), F32),
            pltpu.VMEM((groups - 1, LANES + halves * LANES, edges), BF16),
            pltpu.VMEM((4 * channels, 2 * atoms), BF16),
            pltpu.VMEM((4 * channels, edges), F32),
            pltpu.VMEM((2, 4 * channels, edges), F32),
            pltpu.VMEM((8, channels, atoms), F32),
            pltpu.VMEM((2, 4 * channels, edges), BF16),
            pltpu.VMEM((8, rows * LANES), F32),
            pltpu.VMEM((4, kinds * hidden, atoms), F32),
            pltpu.VMEM((2 * atoms, edges), BF16),
        ]
        + [pltpu.VMEM(p.shape, p.dtype) for p in prepared[1:]]
        + [
            pltpu.SemaphoreType.DMA((len(prepared) + 1,)),
            pltpu.VMEM((groups - 1, 16, LANES), jnp.int32),
            pltpu.VMEM((4 * channels, atoms), F32),
        ],
        compiler_params=pltpu.CompilerParams(vmem_limit_bytes=MAIN_BYTES),
    )(table, neighbours, *prepared)

    if whole:
        returned = lax.all_to_all(grads, AXES, 0, 0, tiled=True)
    else:
        returned = grads.reshape(tuple(window_size(n) for n in dims) + (8, LANES))
        for dim, axis in enumerate(AXES):
            total = None
            for place, step in enumerate(axis_steps(dims[dim])):
                part = lax.slice_in_dim(returned, place, place + 1, axis=dim)
                part = send_along(part, axis, step) if step else part
                total = part if total is None else total + part
            returned = total
        returned = returned.reshape(1, 8, LANES)

    forces = pl.pallas_call(
        functools.partial(forces_kernel, copies),
        out_shape=jax.ShapeDtypeStruct((3, 1, 1, 1, LANES), F32),
        in_specs=[smem, vmem],
        out_specs=vmem,
    )(send_list, returned)
    return (forces.reshape(3, 1, 1, 1, LANES), energy)


def solution(mesh):
    spread = ("groups", "gx")
    return jax.shard_map(
        per_device,
        mesh=mesh,
        in_specs=(
            P(None, spread, "gy", "gz", None),
            P(spread, "gy", "gz", None),
            P(spread, "gy", "gz", None, None),
            P(spread, "gy", "gz", None),
        )
        + (P(),) * 11,
        out_specs=(P(None, spread, "gy", "gz", None), P(spread, "gy", "gz", None)),
        check_vma=False,
    )
```

```python
import functools
import itertools

import jax
import jax.numpy as jnp
from jax import lax
from jax.experimental import pallas as pl
from jax.experimental.pallas import tpu as pltpu
from jax.sharding import PartitionSpec as P

MESSAGE_SCALE = 0.125
CUTOFF_SQUARED = 16.0
AXES = ("gx", "gy", "gz")
LANES = 128
GHOSTS = 16
REACH = 5
VMEM_BYTES = 60 * 1024 * 1024
MAIN_BYTES = 55040 * 1024
F32 = jnp.float32
BF16 = jnp.bfloat16


def window_size(count):
    return min(count, REACH)


def window_place(relative, base, count):
    if count > REACH:
        return relative + 2
    place = relative + base
    for _ in range(2):
        place = jnp.where(place < 0, place + count, place)
    for _ in range(2):
        place = jnp.where(place >= count, place - count, place)
    return place


def near_steps(count):
    return [0, 1, -1][: min(count, 3)]


def near_place(step, count):
    if count >= 3:
        return jnp.where(step < 0, step + 3, step)
    return jnp.where(step == 0, 0, 1)


def split(x):
    high = x.astype(BF16)
    return high, (x - high.astype(F32)).astype(BF16)


def split_wide(x):
    high = x.astype(BF16).astype(F32)
    return high, x - high


def weight_stack(w):
    high, low = split(w)
    return jnp.concatenate([high, low, high], axis=0)


def data_stack(x):
    high, low = split(x)
    return jnp.concatenate([high, high, low], axis=0)


def dot_nn(a, b):
    return lax.dot_general(a, b, (((1,), (0,)), ((), ())), preferred_element_type=F32)


def dot_tn(a, b):
    return lax.dot_general(a, b, (((0,), (0,)), ((), ())), preferred_element_type=F32)


def dot_nt(a, b):
    return lax.dot_general(a, b, (((1,), (1,)), ((), ())), preferred_element_type=F32)


def product_nn(w_high, w_low, x):
    high, low = split(x)
    return dot_nn(w_high, high) + dot_nn(w_low, high) + dot_nn(w_high, low)


def sigmoid(v):
    return 0.5 + 0.5 * jnp.tanh(0.5 * v)


def pick_lanes(row, index):
    return jnp.take_along_axis(jnp.broadcast_to(row, index.shape), index, axis=1)


def iota(shape, dim):
    return lax.broadcasted_iota(jnp.int32, shape, dim)


def pack_kernel(copies, send_ref, pos_ref, species_ref, neigh_ref, out_ref):
    lane = iota((8, LANES), 1)
    row = iota((8, LANES), 0)
    sent = jnp.zeros((8, LANES), jnp.int32)
    for s in range(GHOSTS):
        sent = jnp.where((lane & (GHOSTS - 1)) == s, send_ref[0, 0, 0, s], sent)
    block = jnp.zeros((8, LANES), F32)
    for x in range(3):
        block = jnp.where(row == x, pos_ref[x, 0, 0], block)
    block = jnp.where(row == 3, species_ref[0, 0].astype(F32), block)
    neigh = neigh_ref[0, 0, 0]
    for half in range(2):
        lists = jnp.take_along_axis(neigh[half * 8 : half * 8 + 8], sent, axis=1).astype(F32)
        kept = jnp.where((lane >> 4) == row, lists, 0.0)
        block = jnp.where(row == 4 + half, jnp.sum(kept, axis=0, keepdims=True), block)
    block = jnp.where(row == 6, sent.astype(F32), block)
    for w in range(copies):
        out_ref[w] = block


def forces_kernel(count, send_ref, parts_ref, out_ref):
    total = parts_ref[0]
    for w in range(1, count):
        total = total + parts_ref[w]
    lane = iota((8, LANES), 1)
    slot = jnp.full((8, LANES), -1, jnp.int32)
    for s in range(GHOSTS):
        slot = jnp.where(lane == send_ref[0, 0, 0, s], s, slot)
    moved = jnp.take_along_axis(total, jnp.maximum(slot, 0), axis=1)
    moved = jnp.where(slot >= 0, moved, 0.0)
    for x in range(3):
        out_ref[x, 0, 0] = -(total[x : x + 1] + moved[4 + x : 5 + x])


def decay_rates(basis):
    rates = jnp.zeros((basis, LANES), F32)
    row = iota((basis, LANES), 0)
    for m in range(basis):
        rates = jnp.where(row == m, 0.08 * 2.0 ** (m / 2.0), rates)
    return rates


def ghost_parts(named):
    ghost = jnp.maximum(named - LANES, 0)
    block_id, slot = ghost >> 4, ghost & 15
    first = (block_id * 57) >> 9
    rest = block_id - first * 9
    second = (rest * 11) >> 5
    return [first - 1, second - 1, rest - second * 3 - 1], slot


def wide_stack(w):
    high, low = split(w)
    return jnp.concatenate([high, low, high], axis=1)


def turned_stack(w):
    return wide_stack(jnp.transpose(w))


def prepare_kernel(
    dims,
    neigh_ref,
    embedding_ref,
    win_one_ref,
    wout_one_ref,
    win_two_ref,
    wout_two_ref,
    mss_one_ref,
    msq_one_ref,
    mv_one_ref,
    mss_two_ref,
    msq_two_ref,
    readout_ref,
    pair_ref,
    slots_ref,
    pulls_ref,
    mixes_ref,
    turns_ref,
    paths_ref,
):
    atoms = pair_ref.shape[0]
    basis, hidden = win_one_ref.shape
    kinds, channels = embedding_ref.shape
    near_sizes = [len(near_steps(n)) for n in dims]
    entries = neigh_ref[0, 0, 0]
    named = jnp.maximum(entries, 0)
    shift, slot = ghost_parts(named)
    steps = [near_place(shift[a], dims[a]) for a in range(3)]
    order = (steps[0] * near_sizes[1] + steps[1]) * near_sizes[2] + steps[2]
    row = jnp.where(named < LANES, named, LANES + (order - 1) * GHOSTS + slot)
    row = jnp.where(entries >= 0, row, -1)
    position = iota((atoms, LANES), 0)
    for n in range(16):
        hot = jnp.where(position == row[n : n + 1], 1.0, 0.0).astype(BF16)
        pair_ref[:, n * LANES : (n + 1) * LANES] = hot

    rates = decay_rates(basis)
    for i, win_ref in enumerate((win_one_ref, win_two_ref)):
        win = win_ref[...]
        both = jnp.concatenate([win, -rates[:, :hidden] * win], axis=1)
        high, low = split_wide(both)
        stack = jnp.concatenate([high, high, low, low], axis=0).astype(BF16)
        turns_ref[6, i * 4 * basis : (i + 1) * 4 * basis, 0 : 2 * hidden] = stack
    for j in range(2):
        columns = wout_one_ref[:, j * channels : (j + 1) * channels]
        rows = [columns * embedding_ref[s : s + 1, :] for s in range(kinds)]
        combined = jnp.concatenate(rows, axis=0)
        high, low = split_wide(combined)
        slots_ref[j] = jnp.transpose(jnp.concatenate([high, low, high], axis=0)).astype(BF16)
        pulls_ref[j] = wide_stack(combined)
    pairs = ((mss_one_ref, msq_one_ref), (mss_two_ref, msq_two_ref))
    for i, (scalar_ref, square_ref) in enumerate(pairs):
        mixes_ref[i] = jnp.concatenate(
            [turned_stack(scalar_ref[...]), turned_stack(square_ref[...])], axis=1
        )
        turns_ref[2 + 2 * i] = wide_stack(scalar_ref[...])
        turns_ref[3 + 2 * i] = wide_stack(square_ref[...])
    turns_ref[0] = turned_stack(mv_one_ref[...])
    turns_ref[1] = wide_stack(mv_one_ref[...])
    high, low = split_wide(wout_two_ref[...])
    paths_ref[...] = jnp.transpose(jnp.concatenate([high, low, high], axis=0)).astype(BF16)
    read = jnp.transpose(jnp.broadcast_to(readout_ref[...], (LANES, channels)))
    turns_ref[6, :, LANES : 2 * LANES], turns_ref[6, :, 2 * LANES : 3 * LANES] = split(read)
    lists = jnp.concatenate(split(entries.astype(F32)), axis=0)
    turns_ref[6, 8 * basis : 8 * basis + 32, 0:LANES] = lists
    rest = channels - 8 * basis - 32
    turns_ref[6, channels - rest : channels, 0:LANES] = jnp.zeros((rest, LANES), BF16)


def main_kernel(
    dims,
    near,
    whole,
    rank,
    table_ref,
    pair_hbm,
    slots_hbm,
    pulls_hbm,
    mixes_hbm,
    turns_hbm,
    paths_hbm,
    grad_ref,
    energy_ref,
    r_ref,
    kind_ref,
    dist_ref,
    wh_ref,
    slope_ref,
    wh2_ref,
    moment_ref,
    target_ref,
    feat_ref,
    source_ref,
    radial_ref,
    node_ref,
    dsource_ref,
    dr_ref,
    dmoment_ref,
    pair_ref,
    slots_ref,
    pulls_ref,
    mixes_ref,
    turns_ref,
    paths_ref,
    copy_sem,
    place_ref,
    dfeat_ref,
):
    atoms = pair_hbm.shape[0]
    moves = {}
    for i, (name, source, target) in enumerate(
        (
            ("turns", turns_hbm, turns_ref),
            ("slots", slots_hbm, slots_ref),
            ("mixes", mixes_hbm, mixes_ref),
            ("high", pair_hbm, pair_ref.at[0:atoms]),
            ("low", pair_hbm, pair_ref.at[atoms : 2 * atoms]),
            ("paths", paths_hbm, paths_ref),
            ("pulls", pulls_hbm, pulls_ref),
        )
    ):
        moves[name] = pltpu.make_async_copy(source, target, copy_sem.at[i])
        moves[name].start()

    def ready(*names):
        for name in names:
            moves.pop(name).wait()

    wsize = tuple(window_size(n) for n in dims)
    windows = wsize[0] * wsize[1] * wsize[2]
    halves = -(-windows * GHOSTS // LANES)
    groups = 1 + -(-len(near) // 8)
    channels = LANES
    hidden = paths_ref.shape[1] // 3
    kinds = pulls_ref.shape[1] // hidden
    basis = rank
    own_edges = 16 * LANES

    lane16 = iota((16, LANES), 1)
    sub16 = iota((16, LANES), 0)
    lane8 = iota((8, LANES), 1)
    sub8 = iota((8, LANES), 0)
    bases = [lax.axis_index(axis) if whole else 0 for axis in AXES]
    near_sizes = [len(near_steps(n)) for n in dims]

    def flat(steps):
        places = [window_place(steps[a], bases[a], dims[a]) for a in range(3)]
        return (places[0] * wsize[1] + places[1]) * wsize[2] + places[2]

    own_place = flat((0, 0, 0))
    near_places = [flat(step) for step in near]

    sent = [jnp.zeros((8, LANES), F32) for _ in range(halves)]
    for w in range(windows):
        block = table_ref[w]
        index = jnp.broadcast_to(block[6:7], (8, LANES)).astype(jnp.int32)
        picked = jnp.take_along_axis(block, index, axis=1)
        sent[w // 8] = jnp.where((lane8 >> 4) == w % 8, picked, sent[w // 8])

    for g in [*range(1, groups), 0]:
        members = [] if g == 0 else list(range((g - 1) * 8, min(g * 8, len(near))))
        if g == 0:
            ready("turns")
            lists = turns_ref[6, 8 * rank : 8 * rank + 32, 0:LANES].astype(F32)
            entries = (lists[0:16] + lists[16:32]).astype(jnp.int32)
            own_block = table_ref[own_place]
            centre = [own_block[x : x + 1] for x in range(3)]
            steps = [0, 0, 0]
        else:
            centre8 = jnp.zeros((8, LANES), F32)
            listed = [jnp.full((8, LANES), -1.0, F32) for _ in range(2)]
            steps = [jnp.zeros((16, LANES), jnp.int32) for _ in range(3)]
            for q in members:
                block = table_ref[near_places[q]]
                here = (lane8 >> 4) == q % 8
                index = jnp.broadcast_to(block[6:7], (8, LANES)).astype(jnp.int32)
                centre8 = jnp.where(here, jnp.take_along_axis(block, index, axis=1), centre8)
                for half in range(2):
                    rows = pick_lanes(block[4 + half : 5 + half], sub8 * 16 + (lane8 & 15))
                    listed[half] = jnp.where(here, rows, listed[half])
                for a in range(3):
                    if near[q][a]:
                        steps[a] = jnp.where((lane16 >> 4) == q % 8, near[q][a], steps[a])
            entries = jnp.concatenate(listed, axis=0).astype(jnp.int32)
            centre = [centre8[x : x + 1] for x in range(3)]
        valid = entries >= 0
        named = jnp.maximum(entries, 0)
        local = named < LANES
        local_index = jnp.where(local, named, 0)
        shift, slot = ghost_parts(named)
        sent_index = flat([shift[a] + steps[a] for a in range(3)]) * GHOSTS + slot
        values = []
        for x in range(4):
            if g == 0:
                inside = pick_lanes(own_block[x : x + 1], local_index)
            else:
                inside = jnp.zeros((16, LANES), F32)
                for q in members:
                    rows = pick_lanes(table_ref[near_places[q], x : x + 1, :], local_index)
                    inside = jnp.where((lane16 >> 4) == q % 8, rows, inside)
            outside = jnp.zeros((16, LANES), F32)
            for h in range(halves):
                rows = pick_lanes(sent[h][x : x + 1], sent_index & (LANES - 1))
                outside = jnp.where((sent_index >> 7) == h, rows, outside)
            if x < 3:
                outside = outside + shift[x].astype(F32)
            values.append(jnp.where(local, inside, outside))
        relative = [values[x] - centre[x] for x in range(3)]
        square = relative[0] * relative[0] + relative[1] * relative[1] + relative[2] * relative[2]
        linear = 1.0 - square / CUTOFF_SQUARED
        scale = jnp.where(valid, MESSAGE_SCALE, 0.0)
        dist_ref[0, g * 16 : g * 16 + 16, :] = square
        dist_ref[1, g * 16 : g * 16 + 16, :] = linear * linear * scale
        dist_ref[2, g * 16 : g * 16 + 16, :] = linear * scale * (-2.0 / CUTOFF_SQUARED)
        for n in range(16):
            for x in range(3):
                r_ref[x, g * 16 + n] = jnp.broadcast_to(relative[x][n : n + 1], (8, LANES))
            kind_ref[g * 16 + n] = jnp.broadcast_to(values[3][n : n + 1], (8, LANES))
        if g == 0:
            continue
        row = jnp.where(local, local_index, LANES + sent_index)
        place_ref[g - 1] = jnp.where(valid, row, -1)

    rates = decay_rates(basis)

    def radial_rows(weights, octet):
        dist8 = dist_ref[0, octet * 8 : octet * 8 + 8, :]
        weight8 = dist_ref[1, octet * 8 : octet * 8 + 8, :]
        slope8 = dist_ref[2, octet * 8 : octet * 8 + 8, :]
        values = jnp.concatenate([jnp.exp(-rates * dist8[j : j + 1]) for j in range(8)], axis=1)
        high, low = split_wide(values)
        stacked = jnp.concatenate([high, low, high, low], axis=0).astype(BF16)
        both = dot_tn(weights, stacked)
        rows = []
        for j in range(8):
            before = both[:hidden, j * LANES : (j + 1) * LANES]
            change = both[hidden:, j * LANES : (j + 1) * LANES]
            gate = sigmoid(before)
            after = before * gate
            gain = gate + after * (1.0 - gate)
            weight = weight8[j : j + 1]
            rows.append((weight * after, slope8[j : j + 1] * after + weight * (gain * change)))
        return rows

    def radial_one_step(octet, carry):
        for j, (value, slope) in enumerate(radial_rows(turns_ref[6, 0 : 4 * basis, 0 : 2 * hidden], octet)):
            wh_ref[octet * 8 + j] = value
            slope_ref[octet * 8 + j] = slope
        return carry

    for octet in range(groups * 2):
        radial_one_step(octet, 0)

    def radial_two_step(octet, carry):
        rows = radial_rows(turns_ref[6, 4 * basis : 8 * basis, 0 : 2 * hidden], octet)
        lanes = slice(octet * 8 * LANES, (octet + 1) * 8 * LANES)
        for i in range(2):
            wh2_ref[i, :, lanes] = data_stack(jnp.concatenate([row[i] for row in rows], axis=1))
        return carry

    for octet in range(2):
        radial_two_step(octet, 0)

    def moment_step(step, carry):
        g, part = step // (hidden // 16), step % (hidden // 16)
        lanes = pl.ds(pl.multiple_of(g * LANES, LANES), LANES)
        sums = [[[jnp.zeros((8, LANES), F32) for _ in range(4)] for _ in range(kinds)] for _ in range(2)]
        for n in range(16):
            e = g * 16 + n
            kind = kind_ref[e]
            masks = [kind == float(s) for s in range(kinds)]
            for i in range(2):
                value = wh_ref[e, pl.ds(pl.multiple_of(part * 16 + i * 8, 8), 8), :]
                parts = [value] + [value * r_ref[x, e] for x in range(3)]
                for s in range(kinds):
                    for j in range(4):
                        sums[i][s][j] = sums[i][s][j] + jnp.where(masks[s], parts[j], 0.0)
        for i in range(2):
            for s in range(kinds):
                place = pl.ds(pl.multiple_of(s * hidden + part * 16 + i * 8, 8), 8)
                for j in range(4):
                    moment_ref[j, place, lanes] = sums[i][s][j]
        return carry

    lax.fori_loop(0, groups * (hidden // 16), moment_step, 0)

    ready("slots", "mixes")

    scalar_one = dot_nn(slots_ref[0], data_stack(moment_ref[0]))
    vector_one = [dot_nn(slots_ref[1], data_stack(moment_ref[1 + x])) for x in range(3)]
    squares_one = sum(v * v for v in vector_one)
    before_one = dot_nn(
        mixes_ref[0], jnp.concatenate([data_stack(scalar_one), data_stack(squares_one)], axis=0)
    )
    gate_one = sigmoid(before_one)
    features = [before_one * gate_one] + [dot_nn(turns_ref[0], data_stack(v)) for v in vector_one]
    gain_one = gate_one * (1.0 + before_one * (1.0 - gate_one))
    for j in range(4):
        rows = slice(j * channels, (j + 1) * channels)
        feat_ref[rows, 0:atoms], feat_ref[rows, atoms : 2 * atoms] = split(features[j])
    node_ref[4, :, 0:atoms] = gain_one
    for x in range(3):
        node_ref[5 + x, :, 0:atoms] = vector_one[x]

    ready("high", "low", "paths")

    def edge_step(step, carry):
        lanes = slice(step * 256, step * 256 + 256)
        source_ref[:, lanes] = dot_nn(feat_ref[...], pair_ref[:, lanes])
        for i in range(2):
            radial_ref[i, :, lanes] = dot_nn(paths_ref[...], wh2_ref[i, :, lanes])
        position = iota((LANES + halves * LANES, LANES), 0)
        for i in range(2):
            n = step * 2 + i
            at = slice(n * LANES, n * LANES + LANES)
            for g in range(groups - 1):
                hot = position == place_ref[g, n : n + 1, :]
                target_ref[g, :, at] = jnp.where(hot, 1.0, 0.0).astype(BF16)
        return carry

    def sum_slots(step):
        for part in range(channels // 8):

            def rows(j):
                return slice(j * channels + part * 8, j * channels + part * 8 + 8)

            sums = [node_ref[j, rows(0), 0:LANES] if step else 0.0 for j in range(4)]
            for n in (2 * step, 2 * step + 1):
                lanes = slice(n * LANES, (n + 1) * LANES)
                t = source_ref[rows(0), lanes]
                u = [source_ref[rows(1 + x), lanes] for x in range(3)]
                paths = [radial_ref[0, rows(j), lanes] for j in range(4)]
                r = [r_ref[x, n] for x in range(3)]
                along = r[0] * u[0] + r[1] * u[1] + r[2] * u[2]
                sums[0] = sums[0] + (paths[0] * t + paths[1] * along)
                turned = paths[2] * t
                for x in range(3):
                    sums[1 + x] = sums[1 + x] + (turned * r[x] + paths[3] * u[x])
            for j in range(4):
                node_ref[j, rows(0), 0:LANES] = sums[j]

    for step in range(own_edges // 256):
        edge_step(step, 0)
        if step:
            sum_slots(step - 1)
    sum_slots(own_edges // 256 - 1)


    ready("pulls")

    scalar_two = node_ref[0, :, 0:LANES]
    vector_two = [node_ref[1 + x, :, 0:LANES] for x in range(3)]
    squares_two = sum(v * v for v in vector_two)
    before_two = dot_nn(
        mixes_ref[1], jnp.concatenate([data_stack(scalar_two), data_stack(squares_two)], axis=0)
    )
    gate_two = sigmoid(before_two)
    readout = sum(turns_ref[6, :, i * LANES : (i + 1) * LANES].astype(F32) for i in (1, 2))
    energy_ref[0, 0] = jnp.sum(readout * (before_two * gate_two), axis=0, keepdims=True)
    dbefore_two = readout * (gate_two * (1.0 + before_two * (1.0 - gate_two)))
    dbefore_two = data_stack(dbefore_two)
    dscalar_two = dot_nn(turns_ref[4], dbefore_two)
    dsquares_two = dot_nn(turns_ref[5], dbefore_two)
    node_ref[0, :, 0:LANES] = dscalar_two
    for x in range(3):
        node_ref[1 + x, :, 0:LANES] = 2.0 * vector_two[x] * dsquares_two

    def back_slot(n, half):
        lanes = slice(n * LANES, (n + 1) * LANES)
        r = [jnp.concatenate([r_ref[x, n]] * 2, axis=0) for x in range(3)]
        totals = [jnp.zeros((16, LANES), F32) for _ in range(4)]
        for part in range(half * channels // 32, (half + 1) * channels // 32):

            def rows(j):
                return slice(j * channels + part * 16, j * channels + part * 16 + 16)

            t = source_ref[rows(0), lanes]
            u = [source_ref[rows(1 + x), lanes] for x in range(3)]
            paths = [radial_ref[0, rows(j), lanes] for j in range(4)]
            ds = node_ref[0, rows(0), 0:LANES]
            dv = [node_ref[1 + x, rows(0), 0:LANES] for x in range(3)]
            push = paths[1] * ds
            facing = r[0] * dv[0] + r[1] * dv[1] + r[2] * dv[2]
            along = r[0] * u[0] + r[1] * u[1] + r[2] * u[2]
            meeting = dv[0] * u[0] + dv[1] * u[1] + dv[2] * u[2]
            turned = paths[2] * t
            dsource = [paths[0] * ds + paths[2] * facing]
            for x in range(3):
                dsource.append(push * r[x] + paths[3] * dv[x])
                totals[x] = totals[x] + (push * u[x] + turned * dv[x])
            dradial = [ds * t, ds * along, t * facing, meeting]
            slopes = [radial_ref[1, rows(j), lanes] for j in range(4)]
            products = [dradial[j] * slopes[j] for j in range(4)]
            totals[3] = totals[3] + ((products[0] + products[1]) + (products[2] + products[3]))
            for j in range(4):
                dsource_ref[0, rows(j), lanes], dsource_ref[1, rows(j), lanes] = split(dsource[j])
        dd = 2.0 * jnp.sum(totals[3], axis=0, keepdims=True)
        for x in range(3):
            total = jnp.sum(totals[x], axis=0, keepdims=True) + dd * r_ref[x, n, 0:1, :]
            if half:
                total = total + dr_ref[x : x + 1, lanes]
            dr_ref[x : x + 1, lanes] = total

    for half in range(2):
        for n in range(16):
            back_slot(n, half)
        size = channels // 2
        picked = [slice(j * channels + half * size, j * channels + half * size + size) for j in range(4)]
        stack = [dsource_ref[i, at, :] for i in range(2) for at in picked]
        spread = dot_nt(jnp.concatenate(stack, axis=0), pair_ref[0:atoms, :])
        for j in range(4):
            high = spread[j * size : (j + 1) * size]
            dfeat_ref[picked[j], :] = high + spread[(4 + j) * size : (5 + j) * size]

    dfeat = dfeat_ref[...]
    gain_one = node_ref[4, :, 0:atoms]
    vector_one = [node_ref[5 + x, :, 0:atoms] for x in range(3)]
    dbefore_one = data_stack(dfeat[0:channels] * gain_one)
    dscalar_one = dot_nn(turns_ref[2], dbefore_one)
    dsquares_one = dot_nn(turns_ref[3], dbefore_one)
    dmoment_ref[0] = dot_nn(pulls_ref[0], data_stack(dscalar_one))
    for x in range(3):
        du = data_stack(dfeat[(1 + x) * channels : (2 + x) * channels])
        dvector = 2.0 * vector_one[x] * dsquares_one + dot_nn(turns_ref[1], du)
        dmoment_ref[1 + x] = dot_nn(pulls_ref[1], data_stack(dvector))

    def one_back_step(step, carry):
        g = step // 4
        lanes = pl.ds(pl.multiple_of(g * LANES, LANES), LANES)
        edges = [step * 4 + j for j in range(4)]
        totals = [[jnp.zeros((8, LANES), F32) for _ in range(4)] for _ in range(4)]
        for part in range(hidden // 8):
            rows = slice(part * 8, part * 8 + 8)
            pulls = [
                [dmoment_ref[m, s * hidden + part * 8 : s * hidden + part * 8 + 8, lanes] for m in range(4)]
                for s in range(kinds)
            ]
            for j, e in enumerate(edges):
                kind = kind_ref[e]
                chosen = pulls[0]
                for s in range(1, kinds):
                    mask = kind == float(s)
                    chosen = [jnp.where(mask, pulls[s][m], chosen[m]) for m in range(4)]
                r = [r_ref[x, e] for x in range(3)]
                dwh = chosen[0] + r[0] * chosen[1] + r[1] * chosen[2] + r[2] * chosen[3]
                value = wh_ref[e, rows, :]
                totals[j][3] = totals[j][3] + dwh * slope_ref[e, rows, :]
                for x in range(3):
                    totals[j][x] = totals[j][x] + value * chosen[1 + x]
        for j, e in enumerate(edges):
            at = pl.ds(pl.multiple_of(e * LANES, LANES), LANES)
            dd = 2.0 * jnp.sum(totals[j][3], axis=0, keepdims=True)
            for x in range(3):
                change = jnp.sum(totals[j][x], axis=0, keepdims=True) + dd * r_ref[x, e, 0:1, :]
                dr_ref[4 + x : 5 + x, at] = change
        return carry

    lax.fori_loop(0, groups * 4, one_back_step, 0)

    pieces = []
    for e in range(groups * 16):
        at = slice(e * LANES, (e + 1) * LANES)
        piece = dr_ref[:, at]
        low = pltpu.roll(piece, 4, 0)
        if e < 16:
            piece = jnp.where((sub8 & 3) == 3, 0.0, piece + low)
        else:
            piece = jnp.where((sub8 & 3) == 3, 0.0, jnp.where(sub8 < 4, low, piece))
        pieces.append(piece)
    centres = [sum(pieces[g * 16 : g * 16 + 16]) for g in range(groups)]
    own_change = jnp.concatenate(pieces[:16], axis=1)
    own_high, own_low = split_wide(own_change)
    moved = dot_nt(jnp.concatenate([own_high, own_low], axis=0).astype(BF16), pair_ref[0:atoms, :])
    moved = moved[0:8] + moved[8:16]
    moved = [moved[:, g * LANES : (g + 1) * LANES] - centres[g] for g in range(groups)]

    sent_totals = [jnp.zeros((8, LANES), F32) for _ in range(halves)]
    inner = {}
    for g in range(1, groups):
        members = range((g - 1) * 8, min(g * 8, len(near)))
        change = jnp.concatenate(pieces[g * 16 : g * 16 + 16], axis=1)
        high, low = split_wide(change)
        owner = (iota(change.shape, 1) & (LANES - 1)) >> 4
        stack = [high, low]
        for q in members:
            here = owner == q % 8
            stack += [jnp.where(here, high, 0.0), jnp.where(here, low, 0.0)]
        spread = dot_nt(jnp.concatenate(stack, axis=0).astype(BF16), target_ref[g - 1])
        for h in range(halves):
            lanes = slice(LANES + h * LANES, 2 * LANES + h * LANES)
            sent_totals[h] = sent_totals[h] + (spread[0:8, lanes] + spread[8:16, lanes])
        for i, q in enumerate(members):
            at = 16 + i * 16
            inner[q] = spread[at : at + 8, 0:LANES] + spread[at + 8 : at + 16, 0:LANES]

    spot = lane8 & 15
    for w in range(windows):
        block = jnp.take_along_axis(sent_totals[w // 8], (w % 8) * 16 + spot, axis=1)
        grad_ref[w] = jnp.where(sub8 < 4, 0.0, block)
    grad_ref[own_place] = grad_ref[own_place] + jnp.where(sub8 < 4, moved[0], 0.0)
    for q in range(len(near)):
        block = jnp.take_along_axis(moved[1 + q // 8], (q % 8) * 16 + spot, axis=1)
        grad_ref[near_places[q]] = grad_ref[near_places[q]] + jnp.where(sub8 < 4, inner[q], block)


def send_along(value, axis, steps):
    count = lax.axis_size(axis)
    return lax.ppermute(value, axis, [(i, (i + steps) % count) for i in range(count)])


def axis_steps(count):
    return list(range(count)) if count <= REACH else list(range(-2, 3))


def per_device(
    positions,
    species,
    neighbours,
    send_list,
    embedding,
    radial_in,
    radial_out_one,
    radial_in_two,
    radial_out_two,
    mix_scalar_one,
    mix_square_one,
    mix_vector_one,
    mix_scalar_two,
    mix_square_two,
    readout,
):
    dims = tuple(lax.axis_size(axis) for axis in AXES)
    windows = 1
    for count in dims:
        windows *= window_size(count)
    whole = windows == dims[0] * dims[1] * dims[2] and windows <= 16
    near = [step for step in itertools.product(*[near_steps(n) for n in dims])][1:]
    groups = 1 + -(-len(near) // 8)
    halves = -(-windows * GHOSTS // LANES)
    atoms = groups * LANES
    hidden = radial_in.shape[1]
    kinds, channels = embedding.shape
    copies = windows if whole else 1
    smem = pl.BlockSpec(memory_space=pltpu.SMEM)
    vmem = pl.BlockSpec(memory_space=pltpu.VMEM)

    packed = pl.pallas_call(
        functools.partial(pack_kernel, copies),
        out_shape=jax.ShapeDtypeStruct((copies, 8, LANES), F32),
        in_specs=[smem, vmem, vmem, vmem],
        out_specs=vmem,
    )(send_list, positions, species, neighbours)

    if whole:
        table = lax.all_to_all(packed, AXES, 0, 0, tiled=True)
    else:
        table = packed.reshape(1, 1, 1, 8, LANES)
        for dim, axis in reversed(list(enumerate(AXES))):
            parts = [
                send_along(table, axis, -step) if step else table for step in axis_steps(dims[dim])
            ]
            table = jnp.concatenate(parts, axis=dim)
        table = table.reshape(windows, 8, LANES)

    weights = (
        embedding,
        radial_in,
        radial_out_one,
        radial_in_two,
        radial_out_two,
        mix_scalar_one,
        mix_square_one,
        mix_vector_one,
        mix_scalar_two,
        mix_square_two,
        readout.reshape(1, channels),
    )
    rows = groups * 16
    edges = 16 * LANES
    prepared = pl.pallas_call(
        functools.partial(prepare_kernel, dims),
        out_shape=(
            jax.ShapeDtypeStruct((atoms, edges), BF16),
            jax.ShapeDtypeStruct((2, channels, 3 * kinds * hidden), BF16),
            jax.ShapeDtypeStruct((2, kinds * hidden, 3 * channels), BF16),
            jax.ShapeDtypeStruct((2, channels, 6 * channels), BF16),
            jax.ShapeDtypeStruct((7, channels, 3 * channels), BF16),
            jax.ShapeDtypeStruct((4 * channels, 3 * hidden), BF16),
        ),
        in_specs=[vmem] * 12,
        out_specs=(vmem,) * 6,
        compiler_params=pltpu.CompilerParams(vmem_limit_bytes=VMEM_BYTES),
        cost_estimate=pl.CostEstimate(flops=0, bytes_accessed=8 * 1024 * 1024, transcendentals=0),
    )(neighbours, *weights)
    grads, energy = pl.pallas_call(
        functools.partial(main_kernel, dims, near, whole, radial_in.shape[0]),
        out_shape=(
            jax.ShapeDtypeStruct((windows, 8, LANES), F32),
            jax.ShapeDtypeStruct((1, 1, 1, LANES), F32),
        ),
        in_specs=[vmem] + [pl.BlockSpec(memory_space=pltpu.HBM)] * len(prepared),
        out_specs=(vmem, vmem),
        scratch_shapes=[
            pltpu.VMEM((3, rows, 8, LANES), F32),
            pltpu.VMEM((rows, 8, LANES), F32),
            pltpu.VMEM((3, rows, LANES), F32),
            pltpu.VMEM((rows, hidden, LANES), F32),
            pltpu.VMEM((rows, hidden, LANES), F32),
            pltpu.VMEM((2, 3 * hidden, edges), BF16),
            pltpu.VMEM((4, kinds * hidden, atoms), F32),
            pltpu.VMEM((groups - 1, LANES + halves * LANES, edges), BF16),
            pltpu.VMEM((4 * channels, 2 * atoms), BF16),
            pltpu.VMEM((4 * channels, edges), F32),
            pltpu.VMEM((2, 4 * channels, edges), F32),
            pltpu.VMEM((8, channels, atoms), F32),
            pltpu.VMEM((2, 4 * channels, edges), BF16),
            pltpu.VMEM((8, rows * LANES), F32),
            pltpu.VMEM((4, kinds * hidden, atoms), F32),
            pltpu.VMEM((2 * atoms, edges), BF16),
        ]
        + [pltpu.VMEM(p.shape, p.dtype) for p in prepared[1:]]
        + [
            pltpu.SemaphoreType.DMA((len(prepared) + 1,)),
            pltpu.VMEM((groups - 1, 16, LANES), jnp.int32),
            pltpu.VMEM((4 * channels, atoms), F32),
        ],
        compiler_params=pltpu.CompilerParams(vmem_limit_bytes=MAIN_BYTES),
    )(table, *prepared)

    if whole:
        returned = lax.all_to_all(grads, AXES, 0, 0, tiled=True)
    else:
        returned = grads.reshape(tuple(window_size(n) for n in dims) + (8, LANES))
        for dim, axis in enumerate(AXES):
            total = None
            for place, step in enumerate(axis_steps(dims[dim])):
                part = lax.slice_in_dim(returned, place, place + 1, axis=dim)
                part = send_along(part, axis, step) if step else part
                total = part if total is None else total + part
            returned = total
        returned = returned.reshape(1, 8, LANES)

    forces = pl.pallas_call(
        functools.partial(forces_kernel, copies),
        out_shape=jax.ShapeDtypeStruct((3, 1, 1, 1, LANES), F32),
        in_specs=[smem, vmem],
        out_specs=vmem,
    )(send_list, returned)
    return (forces.reshape(3, 1, 1, 1, LANES), energy)


def solution(mesh):
    spread = ("groups", "gx")
    return jax.shard_map(
        per_device,
        mesh=mesh,
        in_specs=(
            P(None, spread, "gy", "gz", None),
            P(spread, "gy", "gz", None),
            P(spread, "gy", "gz", None, None),
            P(spread, "gy", "gz", None),
        )
        + (P(),) * 11,
        out_specs=(P(None, spread, "gy", "gz", None), P(spread, "gy", "gz", None)),
        check_vma=False,
    )
```

```python
import functools
import itertools

import jax
import jax.numpy as jnp
from jax import lax
from jax.experimental import pallas as pl
from jax.experimental.pallas import tpu as pltpu
from jax.sharding import PartitionSpec as P

MESSAGE_SCALE = 0.125
CUTOFF_SQUARED = 16.0
AXES = ("gx", "gy", "gz")
LANES = 128
GHOSTS = 16
REACH = 5
VMEM_BYTES = 60 * 1024 * 1024
MAIN_BYTES = 55040 * 1024
F32 = jnp.float32
BF16 = jnp.bfloat16


def window_size(count):
    return min(count, REACH)


def window_place(relative, base, count):
    if count > REACH:
        return relative + 2
    place = relative + base
    for _ in range(2):
        place = jnp.where(place < 0, place + count, place)
    for _ in range(2):
        place = jnp.where(place >= count, place - count, place)
    return place


def near_steps(count):
    return [0, 1, -1][: min(count, 3)]


def near_place(step, count):
    if count >= 3:
        return jnp.where(step < 0, step + 3, step)
    return jnp.where(step == 0, 0, 1)


def split(x):
    high = x.astype(BF16)
    return high, (x - high.astype(F32)).astype(BF16)


def split_wide(x):
    high = x.astype(BF16).astype(F32)
    return high, x - high


def weight_stack(w):
    high, low = split(w)
    return jnp.concatenate([high, low, high], axis=0)


def data_stack(x):
    high, low = split(x)
    return jnp.concatenate([high, high, low], axis=0)


def dot_nn(a, b):
    return lax.dot_general(a, b, (((1,), (0,)), ((), ())), preferred_element_type=F32)


def dot_tn(a, b):
    return lax.dot_general(a, b, (((0,), (0,)), ((), ())), preferred_element_type=F32)


def dot_nt(a, b):
    return lax.dot_general(a, b, (((1,), (1,)), ((), ())), preferred_element_type=F32)


def product_nn(w_high, w_low, x):
    high, low = split(x)
    return dot_nn(w_high, high) + dot_nn(w_low, high) + dot_nn(w_high, low)


def sigmoid(v):
    return 0.5 + 0.5 * jnp.tanh(0.5 * v)


def pick_lanes(row, index):
    return jnp.take_along_axis(jnp.broadcast_to(row, index.shape), index, axis=1)


def iota(shape, dim):
    return lax.broadcasted_iota(jnp.int32, shape, dim)


def pack_kernel(copies, send_ref, pos_ref, species_ref, neigh_ref, out_ref):
    lane = iota((8, LANES), 1)
    row = iota((8, LANES), 0)
    sent = jnp.zeros((8, LANES), jnp.int32)
    for s in range(GHOSTS):
        sent = jnp.where((lane & (GHOSTS - 1)) == s, send_ref[0, 0, 0, s], sent)
    block = jnp.zeros((8, LANES), F32)
    for x in range(3):
        block = jnp.where(row == x, pos_ref[x, 0, 0], block)
    block = jnp.where(row == 3, species_ref[0, 0].astype(F32), block)
    neigh = neigh_ref[0, 0, 0]
    for half in range(2):
        lists = jnp.take_along_axis(neigh[half * 8 : half * 8 + 8], sent, axis=1).astype(F32)
        kept = jnp.where((lane >> 4) == row, lists, 0.0)
        block = jnp.where(row == 4 + half, jnp.sum(kept, axis=0, keepdims=True), block)
    block = jnp.where(row == 6, sent.astype(F32), block)
    for w in range(copies):
        out_ref[w] = block


def forces_kernel(count, send_ref, parts_ref, out_ref):
    total = parts_ref[0]
    for w in range(1, count):
        total = total + parts_ref[w]
    lane = iota((8, LANES), 1)
    slot = jnp.full((8, LANES), -1, jnp.int32)
    for s in range(GHOSTS):
        slot = jnp.where(lane == send_ref[0, 0, 0, s], s, slot)
    moved = jnp.take_along_axis(total, jnp.maximum(slot, 0), axis=1)
    moved = jnp.where(slot >= 0, moved, 0.0)
    for x in range(3):
        out_ref[x, 0, 0] = -(total[x : x + 1] + moved[4 + x : 5 + x])


def decay_rates(basis):
    rates = jnp.zeros((basis, LANES), F32)
    row = iota((basis, LANES), 0)
    for m in range(basis):
        rates = jnp.where(row == m, 0.08 * 2.0 ** (m / 2.0), rates)
    return rates


def ghost_parts(named):
    ghost = jnp.maximum(named - LANES, 0)
    block_id, slot = ghost >> 4, ghost & 15
    first = (block_id * 57) >> 9
    rest = block_id - first * 9
    second = (rest * 11) >> 5
    return [first - 1, second - 1, rest - second * 3 - 1], slot


def wide_stack(w):
    high, low = split(w)
    return jnp.concatenate([high, low, high], axis=1)


def turned_stack(w):
    return wide_stack(jnp.transpose(w))


def prepare_kernel(
    dims,
    neigh_ref,
    embedding_ref,
    win_one_ref,
    wout_one_ref,
    win_two_ref,
    wout_two_ref,
    mss_one_ref,
    msq_one_ref,
    mv_one_ref,
    mss_two_ref,
    msq_two_ref,
    readout_ref,
    pair_ref,
    slots_ref,
    pulls_ref,
    mixes_ref,
    turns_ref,
    paths_ref,
):
    atoms = pair_ref.shape[0]
    basis, hidden = win_one_ref.shape
    kinds, channels = embedding_ref.shape
    near_sizes = [len(near_steps(n)) for n in dims]
    entries = neigh_ref[0, 0, 0]
    named = jnp.maximum(entries, 0)
    shift, slot = ghost_parts(named)
    steps = [near_place(shift[a], dims[a]) for a in range(3)]
    order = (steps[0] * near_sizes[1] + steps[1]) * near_sizes[2] + steps[2]
    row = jnp.where(named < LANES, named, LANES + (order - 1) * GHOSTS + slot)
    row = jnp.where(entries >= 0, row, -1)
    position = iota((atoms, LANES), 0)
    for n in range(16):
        hot = jnp.where(position == row[n : n + 1], 1.0, 0.0).astype(BF16)
        pair_ref[:, n * LANES : (n + 1) * LANES] = hot

    rates = decay_rates(basis)
    for i, win_ref in enumerate((win_one_ref, win_two_ref)):
        win = win_ref[...]
        both = jnp.concatenate([win, -rates[:, :hidden] * win], axis=1)
        high, low = split_wide(both)
        stack = jnp.concatenate([high, high, low, low], axis=0).astype(BF16)
        turns_ref[6, i * 4 * basis : (i + 1) * 4 * basis, 0 : 2 * hidden] = stack
    for j in range(2):
        columns = wout_one_ref[:, j * channels : (j + 1) * channels]
        rows = [columns * embedding_ref[s : s + 1, :] for s in range(kinds)]
        combined = jnp.concatenate(rows, axis=0)
        high, low = split_wide(combined)
        slots_ref[j] = jnp.transpose(jnp.concatenate([high, low, high], axis=0)).astype(BF16)
        pulls_ref[j] = wide_stack(combined)
    pairs = ((mss_one_ref, msq_one_ref), (mss_two_ref, msq_two_ref))
    for i, (scalar_ref, square_ref) in enumerate(pairs):
        mixes_ref[i] = jnp.concatenate(
            [turned_stack(scalar_ref[...]), turned_stack(square_ref[...])], axis=1
        )
        turns_ref[2 + 2 * i] = wide_stack(scalar_ref[...])
        turns_ref[3 + 2 * i] = wide_stack(square_ref[...])
    turns_ref[0] = turned_stack(mv_one_ref[...])
    turns_ref[1] = wide_stack(mv_one_ref[...])
    high, low = split_wide(wout_two_ref[...])
    paths_ref[...] = jnp.transpose(jnp.concatenate([high, low, high], axis=0)).astype(BF16)
    read = jnp.transpose(jnp.broadcast_to(readout_ref[...], (LANES, channels)))
    turns_ref[6, :, LANES : 2 * LANES], turns_ref[6, :, 2 * LANES : 3 * LANES] = split(read)
    lists = jnp.concatenate(split(entries.astype(F32)), axis=0)
    turns_ref[6, 8 * basis : 8 * basis + 32, 0:LANES] = lists
    rest = channels - 8 * basis - 32
    turns_ref[6, channels - rest : channels, 0:LANES] = jnp.zeros((rest, LANES), BF16)


def main_kernel(
    dims,
    near,
    whole,
    rank,
    table_ref,
    pair_hbm,
    slots_hbm,
    pulls_hbm,
    mixes_hbm,
    turns_hbm,
    paths_hbm,
    grad_ref,
    energy_ref,
    r_ref,
    kind_ref,
    dist_ref,
    wh_ref,
    slope_ref,
    wh2_ref,
    moment_ref,
    target_ref,
    feat_ref,
    source_ref,
    radial_ref,
    node_ref,
    dsource_ref,
    dr_ref,
    dmoment_ref,
    pair_ref,
    slots_ref,
    pulls_ref,
    mixes_ref,
    turns_ref,
    paths_ref,
    copy_sem,
    place_ref,
    dfeat_ref,
):
    atoms = pair_hbm.shape[0]
    moves = {}
    for i, (name, source, target) in enumerate(
        (
            ("turns", turns_hbm, turns_ref),
            ("slots", slots_hbm, slots_ref),
            ("mixes", mixes_hbm, mixes_ref),
            ("high", pair_hbm, pair_ref.at[0:atoms]),
            ("low", pair_hbm, pair_ref.at[atoms : 2 * atoms]),
            ("paths", paths_hbm, paths_ref),
            ("pulls", pulls_hbm, pulls_ref),
        )
    ):
        moves[name] = pltpu.make_async_copy(source, target, copy_sem.at[i])
        moves[name].start()

    def ready(*names):
        for name in names:
            moves.pop(name).wait()

    wsize = tuple(window_size(n) for n in dims)
    windows = wsize[0] * wsize[1] * wsize[2]
    halves = -(-windows * GHOSTS // LANES)
    groups = 1 + -(-len(near) // 8)
    channels = LANES
    hidden = paths_ref.shape[1] // 3
    kinds = pulls_ref.shape[1] // hidden
    basis = rank
    own_edges = 16 * LANES

    lane16 = iota((16, LANES), 1)
    sub16 = iota((16, LANES), 0)
    lane8 = iota((8, LANES), 1)
    sub8 = iota((8, LANES), 0)
    bases = [lax.axis_index(axis) if whole else 0 for axis in AXES]
    near_sizes = [len(near_steps(n)) for n in dims]

    def flat(steps):
        places = [window_place(steps[a], bases[a], dims[a]) for a in range(3)]
        return (places[0] * wsize[1] + places[1]) * wsize[2] + places[2]

    own_place = flat((0, 0, 0))
    near_places = [flat(step) for step in near]

    sent = [jnp.zeros((8, LANES), F32) for _ in range(halves)]
    for w in range(windows):
        block = table_ref[w]
        index = jnp.broadcast_to(block[6:7], (8, LANES)).astype(jnp.int32)
        picked = jnp.take_along_axis(block, index, axis=1)
        sent[w // 8] = jnp.where((lane8 >> 4) == w % 8, picked, sent[w // 8])

    for g in [*range(1, groups), 0]:
        members = [] if g == 0 else list(range((g - 1) * 8, min(g * 8, len(near))))
        if g == 0:
            ready("turns")
            lists = turns_ref[6, 8 * rank : 8 * rank + 32, 0:LANES].astype(F32)
            entries = (lists[0:16] + lists[16:32]).astype(jnp.int32)
            own_block = table_ref[own_place]
            centre = [own_block[x : x + 1] for x in range(3)]
            steps = [0, 0, 0]
        else:
            centre8 = jnp.zeros((8, LANES), F32)
            listed = [jnp.full((8, LANES), -1.0, F32) for _ in range(2)]
            steps = [jnp.zeros((16, LANES), jnp.int32) for _ in range(3)]
            for q in members:
                block = table_ref[near_places[q]]
                here = (lane8 >> 4) == q % 8
                index = jnp.broadcast_to(block[6:7], (8, LANES)).astype(jnp.int32)
                centre8 = jnp.where(here, jnp.take_along_axis(block, index, axis=1), centre8)
                for half in range(2):
                    rows = pick_lanes(block[4 + half : 5 + half], sub8 * 16 + (lane8 & 15))
                    listed[half] = jnp.where(here, rows, listed[half])
                for a in range(3):
                    if near[q][a]:
                        steps[a] = jnp.where((lane16 >> 4) == q % 8, near[q][a], steps[a])
            entries = jnp.concatenate(listed, axis=0).astype(jnp.int32)
            centre = [centre8[x : x + 1] for x in range(3)]
        valid = entries >= 0
        named = jnp.maximum(entries, 0)
        local = named < LANES
        local_index = jnp.where(local, named, 0)
        shift, slot = ghost_parts(named)
        sent_index = flat([shift[a] + steps[a] for a in range(3)]) * GHOSTS + slot
        values = []
        for x in range(4):
            if g == 0:
                inside = pick_lanes(own_block[x : x + 1], local_index)
            else:
                inside = jnp.zeros((16, LANES), F32)
                for q in members:
                    rows = pick_lanes(table_ref[near_places[q], x : x + 1, :], local_index)
                    inside = jnp.where((lane16 >> 4) == q % 8, rows, inside)
            outside = jnp.zeros((16, LANES), F32)
            for h in range(halves):
                rows = pick_lanes(sent[h][x : x + 1], sent_index & (LANES - 1))
                outside = jnp.where((sent_index >> 7) == h, rows, outside)
            if x < 3:
                outside = outside + shift[x].astype(F32)
            values.append(jnp.where(local, inside, outside))
        relative = [values[x] - centre[x] for x in range(3)]
        square = relative[0] * relative[0] + relative[1] * relative[1] + relative[2] * relative[2]
        linear = 1.0 - square / CUTOFF_SQUARED
        scale = jnp.where(valid, MESSAGE_SCALE, 0.0)
        dist_ref[0, g * 16 : g * 16 + 16, :] = square
        dist_ref[1, g * 16 : g * 16 + 16, :] = linear * linear * scale
        dist_ref[2, g * 16 : g * 16 + 16, :] = linear * scale * (-2.0 / CUTOFF_SQUARED)
        for n in range(16):
            for x in range(3):
                r_ref[x, g * 16 + n] = jnp.broadcast_to(relative[x][n : n + 1], (8, LANES))
            kind_ref[g * 16 + n] = jnp.broadcast_to(values[3][n : n + 1], (8, LANES))
        if g == 0:
            continue
        row = jnp.where(local, local_index, LANES + sent_index)
        place_ref[g - 1] = jnp.where(valid, row, -1)

    rates = decay_rates(basis)

    def radial_rows(weights, octet):
        dist8 = dist_ref[0, octet * 8 : octet * 8 + 8, :]
        weight8 = dist_ref[1, octet * 8 : octet * 8 + 8, :]
        slope8 = dist_ref[2, octet * 8 : octet * 8 + 8, :]
        values = jnp.concatenate([jnp.exp(-rates * dist8[j : j + 1]) for j in range(8)], axis=1)
        high, low = split_wide(values)
        stacked = jnp.concatenate([high, low, high, low], axis=0).astype(BF16)
        both = dot_tn(weights, stacked)
        rows = []
        for j in range(8):
            before = both[:hidden, j * LANES : (j + 1) * LANES]
            change = both[hidden:, j * LANES : (j + 1) * LANES]
            gate = sigmoid(before)
            after = before * gate
            gain = gate + after * (1.0 - gate)
            weight = weight8[j : j + 1]
            rows.append((weight * after, slope8[j : j + 1] * after + weight * (gain * change)))
        return rows

    def radial_one_step(octet, carry):
        for j, (value, slope) in enumerate(radial_rows(turns_ref[6, 0 : 4 * basis, 0 : 2 * hidden], octet)):
            wh_ref[octet * 8 + j] = value
            slope_ref[octet * 8 + j] = slope
        return carry

    for octet in range(groups * 2):
        radial_one_step(octet, 0)

    def radial_two_step(octet, carry):
        rows = radial_rows(turns_ref[6, 4 * basis : 8 * basis, 0 : 2 * hidden], octet)
        lanes = slice(octet * 8 * LANES, (octet + 1) * 8 * LANES)
        for i in range(2):
            wh2_ref[i, :, lanes] = data_stack(jnp.concatenate([row[i] for row in rows], axis=1))
        return carry

    for octet in range(2):
        radial_two_step(octet, 0)

    def moment_step(step, carry):
        g, part = step // (hidden // 16), step % (hidden // 16)
        lanes = pl.ds(pl.multiple_of(g * LANES, LANES), LANES)
        sums = [[[jnp.zeros((8, LANES), F32) for _ in range(4)] for _ in range(kinds)] for _ in range(2)]
        for n in range(16):
            e = g * 16 + n
            kind = kind_ref[e]
            masks = [kind == float(s) for s in range(kinds - 1)]
            for i in range(2):
                value = wh_ref[e, pl.ds(pl.multiple_of(part * 16 + i * 8, 8), 8), :]
                parts = [value] + [value * r_ref[x, e] for x in range(3)]
                for j in range(4):
                    sums[i][-1][j] = sums[i][-1][j] + parts[j]
                    for s in range(kinds - 1):
                        sums[i][s][j] = sums[i][s][j] + jnp.where(masks[s], parts[j], 0.0)
        for i in range(2):
            for j in range(4):
                sums[i][-1][j] = sums[i][-1][j] - sum(sums[i][s][j] for s in range(kinds - 1))
            for s in range(kinds):
                place = pl.ds(pl.multiple_of(s * hidden + part * 16 + i * 8, 8), 8)
                for j in range(4):
                    moment_ref[j, place, lanes] = sums[i][s][j]
        return carry

    lax.fori_loop(0, groups * (hidden // 16), moment_step, 0)

    ready("slots", "mixes")

    scalar_one = dot_nn(slots_ref[0], data_stack(moment_ref[0]))
    vector_one = [dot_nn(slots_ref[1], data_stack(moment_ref[1 + x])) for x in range(3)]
    squares_one = sum(v * v for v in vector_one)
    before_one = dot_nn(
        mixes_ref[0], jnp.concatenate([data_stack(scalar_one), data_stack(squares_one)], axis=0)
    )
    gate_one = sigmoid(before_one)
    features = [before_one * gate_one] + [dot_nn(turns_ref[0], data_stack(v)) for v in vector_one]
    gain_one = gate_one * (1.0 + before_one * (1.0 - gate_one))
    for j in range(4):
        rows = slice(j * channels, (j + 1) * channels)
        feat_ref[rows, 0:atoms], feat_ref[rows, atoms : 2 * atoms] = split(features[j])
    node_ref[4, :, 0:atoms] = gain_one
    for x in range(3):
        node_ref[5 + x, :, 0:atoms] = vector_one[x]

    ready("high", "low", "paths")

    def edge_step(step, carry):
        lanes = slice(step * 256, step * 256 + 256)
        source_ref[:, lanes] = dot_nn(feat_ref[...], pair_ref[:, lanes])
        for i in range(2):
            radial_ref[i, :, lanes] = dot_nn(paths_ref[...], wh2_ref[i, :, lanes])
        position = iota((LANES + halves * LANES, LANES), 0)
        for i in range(2):
            n = step * 2 + i
            at = slice(n * LANES, n * LANES + LANES)
            for g in range(groups - 1):
                hot = position == place_ref[g, n : n + 1, :]
                target_ref[g, :, at] = jnp.where(hot, 1.0, 0.0).astype(BF16)
        return carry

    def sum_slots(step):
        for part in range(channels // 8):

            def rows(j):
                return slice(j * channels + part * 8, j * channels + part * 8 + 8)

            sums = [node_ref[j, rows(0), 0:LANES] if step else 0.0 for j in range(4)]
            for n in (2 * step, 2 * step + 1):
                lanes = slice(n * LANES, (n + 1) * LANES)
                t = source_ref[rows(0), lanes]
                u = [source_ref[rows(1 + x), lanes] for x in range(3)]
                paths = [radial_ref[0, rows(j), lanes] for j in range(4)]
                r = [r_ref[x, n] for x in range(3)]
                along = r[0] * u[0] + r[1] * u[1] + r[2] * u[2]
                sums[0] = sums[0] + (paths[0] * t + paths[1] * along)
                turned = paths[2] * t
                for x in range(3):
                    sums[1 + x] = sums[1 + x] + (turned * r[x] + paths[3] * u[x])
            for j in range(4):
                node_ref[j, rows(0), 0:LANES] = sums[j]

    for step in range(own_edges // 256):
        edge_step(step, 0)
        if step:
            sum_slots(step - 1)
    sum_slots(own_edges // 256 - 1)


    ready("pulls")

    scalar_two = node_ref[0, :, 0:LANES]
    vector_two = [node_ref[1 + x, :, 0:LANES] for x in range(3)]
    squares_two = sum(v * v for v in vector_two)
    before_two = dot_nn(
        mixes_ref[1], jnp.concatenate([data_stack(scalar_two), data_stack(squares_two)], axis=0)
    )
    gate_two = sigmoid(before_two)
    readout = sum(turns_ref[6, :, i * LANES : (i + 1) * LANES].astype(F32) for i in (1, 2))
    energy_ref[0, 0] = jnp.sum(readout * (before_two * gate_two), axis=0, keepdims=True)
    dbefore_two = readout * (gate_two * (1.0 + before_two * (1.0 - gate_two)))
    dbefore_two = data_stack(dbefore_two)
    dscalar_two = dot_nn(turns_ref[4], dbefore_two)
    dsquares_two = dot_nn(turns_ref[5], dbefore_two)
    node_ref[0, :, 0:LANES] = dscalar_two
    for x in range(3):
        node_ref[1 + x, :, 0:LANES] = 2.0 * vector_two[x] * dsquares_two

    def back_slot(n, half):
        lanes = slice(n * LANES, (n + 1) * LANES)
        r = [jnp.concatenate([r_ref[x, n]] * 2, axis=0) for x in range(3)]
        totals = [jnp.zeros((16, LANES), F32) for _ in range(4)]
        for part in range(half * channels // 32, (half + 1) * channels // 32):

            def rows(j):
                return slice(j * channels + part * 16, j * channels + part * 16 + 16)

            t = source_ref[rows(0), lanes]
            u = [source_ref[rows(1 + x), lanes] for x in range(3)]
            paths = [radial_ref[0, rows(j), lanes] for j in range(4)]
            ds = node_ref[0, rows(0), 0:LANES]
            dv = [node_ref[1 + x, rows(0), 0:LANES] for x in range(3)]
            push = paths[1] * ds
            facing = r[0] * dv[0] + r[1] * dv[1] + r[2] * dv[2]
            along = r[0] * u[0] + r[1] * u[1] + r[2] * u[2]
            meeting = dv[0] * u[0] + dv[1] * u[1] + dv[2] * u[2]
            turned = paths[2] * t
            dsource = [paths[0] * ds + paths[2] * facing]
            for x in range(3):
                dsource.append(push * r[x] + paths[3] * dv[x])
                totals[x] = totals[x] + (push * u[x] + turned * dv[x])
            dradial = [ds * t, ds * along, t * facing, meeting]
            slopes = [radial_ref[1, rows(j), lanes] for j in range(4)]
            products = [dradial[j] * slopes[j] for j in range(4)]
            totals[3] = totals[3] + ((products[0] + products[1]) + (products[2] + products[3]))
            for j in range(4):
                dsource_ref[0, rows(j), lanes], dsource_ref[1, rows(j), lanes] = split(dsource[j])
        dd = 2.0 * jnp.sum(totals[3], axis=0, keepdims=True)
        for x in range(3):
            total = jnp.sum(totals[x], axis=0, keepdims=True) + dd * r_ref[x, n, 0:1, :]
            if half:
                total = total + dr_ref[x : x + 1, lanes]
            dr_ref[x : x + 1, lanes] = total

    for half in range(2):
        for n in range(16):
            back_slot(n, half)
        size = channels // 2
        picked = [slice(j * channels + half * size, j * channels + half * size + size) for j in range(4)]
        stack = [dsource_ref[i, at, :] for i in range(2) for at in picked]
        spread = dot_nt(jnp.concatenate(stack, axis=0), pair_ref[0:atoms, :])
        for j in range(4):
            high = spread[j * size : (j + 1) * size]
            dfeat_ref[picked[j], :] = high + spread[(4 + j) * size : (5 + j) * size]

    dfeat = dfeat_ref[...]
    gain_one = node_ref[4, :, 0:atoms]
    vector_one = [node_ref[5 + x, :, 0:atoms] for x in range(3)]
    dbefore_one = data_stack(dfeat[0:channels] * gain_one)
    dscalar_one = dot_nn(turns_ref[2], dbefore_one)
    dsquares_one = dot_nn(turns_ref[3], dbefore_one)
    dmoment_ref[0] = dot_nn(pulls_ref[0], data_stack(dscalar_one))
    for x in range(3):
        du = data_stack(dfeat[(1 + x) * channels : (2 + x) * channels])
        dvector = 2.0 * vector_one[x] * dsquares_one + dot_nn(turns_ref[1], du)
        dmoment_ref[1 + x] = dot_nn(pulls_ref[1], data_stack(dvector))

    def one_back_step(step, carry):
        g = step // 4
        lanes = pl.ds(pl.multiple_of(g * LANES, LANES), LANES)
        edges = [step * 4 + j for j in range(4)]
        totals = [[jnp.zeros((8, LANES), F32) for _ in range(4)] for _ in range(4)]
        for part in range(hidden // 8):
            rows = slice(part * 8, part * 8 + 8)
            pulls = [
                [dmoment_ref[m, s * hidden + part * 8 : s * hidden + part * 8 + 8, lanes] for m in range(4)]
                for s in range(kinds)
            ]
            for j, e in enumerate(edges):
                kind = kind_ref[e]
                chosen = pulls[0]
                for s in range(1, kinds):
                    mask = kind == float(s)
                    chosen = [jnp.where(mask, pulls[s][m], chosen[m]) for m in range(4)]
                r = [r_ref[x, e] for x in range(3)]
                dwh = chosen[0] + r[0] * chosen[1] + r[1] * chosen[2] + r[2] * chosen[3]
                value = wh_ref[e, rows, :]
                totals[j][3] = totals[j][3] + dwh * slope_ref[e, rows, :]
                for x in range(3):
                    totals[j][x] = totals[j][x] + value * chosen[1 + x]
        for j, e in enumerate(edges):
            at = pl.ds(pl.multiple_of(e * LANES, LANES), LANES)
            dd = 2.0 * jnp.sum(totals[j][3], axis=0, keepdims=True)
            for x in range(3):
                change = jnp.sum(totals[j][x], axis=0, keepdims=True) + dd * r_ref[x, e, 0:1, :]
                dr_ref[4 + x : 5 + x, at] = change
        return carry

    lax.fori_loop(0, groups * 4, one_back_step, 0)

    pieces = []
    for e in range(groups * 16):
        at = slice(e * LANES, (e + 1) * LANES)
        piece = dr_ref[:, at]
        low = pltpu.roll(piece, 4, 0)
        if e < 16:
            piece = jnp.where((sub8 & 3) == 3, 0.0, piece + low)
        else:
            piece = jnp.where((sub8 & 3) == 3, 0.0, jnp.where(sub8 < 4, low, piece))
        pieces.append(piece)
    centres = [sum(pieces[g * 16 : g * 16 + 16]) for g in range(groups)]
    own_change = jnp.concatenate(pieces[:16], axis=1)
    own_high, own_low = split_wide(own_change)
    moved = dot_nt(jnp.concatenate([own_high, own_low], axis=0).astype(BF16), pair_ref[0:atoms, :])
    moved = moved[0:8] + moved[8:16]
    moved = [moved[:, g * LANES : (g + 1) * LANES] - centres[g] for g in range(groups)]

    sent_totals = [jnp.zeros((8, LANES), F32) for _ in range(halves)]
    inner = {}
    for g in range(1, groups):
        members = range((g - 1) * 8, min(g * 8, len(near)))
        change = jnp.concatenate(pieces[g * 16 : g * 16 + 16], axis=1)
        high, low = split_wide(change)
        owner = (iota(change.shape, 1) & (LANES - 1)) >> 4
        stack = [high, low]
        for q in members:
            here = owner == q % 8
            stack += [jnp.where(here, high, 0.0), jnp.where(here, low, 0.0)]
        spread = dot_nt(jnp.concatenate(stack, axis=0).astype(BF16), target_ref[g - 1])
        for h in range(halves):
            lanes = slice(LANES + h * LANES, 2 * LANES + h * LANES)
            sent_totals[h] = sent_totals[h] + (spread[0:8, lanes] + spread[8:16, lanes])
        for i, q in enumerate(members):
            at = 16 + i * 16
            inner[q] = spread[at : at + 8, 0:LANES] + spread[at + 8 : at + 16, 0:LANES]

    spot = lane8 & 15
    for w in range(windows):
        block = jnp.take_along_axis(sent_totals[w // 8], (w % 8) * 16 + spot, axis=1)
        grad_ref[w] = jnp.where(sub8 < 4, 0.0, block)
    grad_ref[own_place] = grad_ref[own_place] + jnp.where(sub8 < 4, moved[0], 0.0)
    for q in range(len(near)):
        block = jnp.take_along_axis(moved[1 + q // 8], (q % 8) * 16 + spot, axis=1)
        grad_ref[near_places[q]] = grad_ref[near_places[q]] + jnp.where(sub8 < 4, inner[q], block)


def send_along(value, axis, steps):
    count = lax.axis_size(axis)
    return lax.ppermute(value, axis, [(i, (i + steps) % count) for i in range(count)])


def axis_steps(count):
    return list(range(count)) if count <= REACH else list(range(-2, 3))


def per_device(
    positions,
    species,
    neighbours,
    send_list,
    embedding,
    radial_in,
    radial_out_one,
    radial_in_two,
    radial_out_two,
    mix_scalar_one,
    mix_square_one,
    mix_vector_one,
    mix_scalar_two,
    mix_square_two,
    readout,
):
    dims = tuple(lax.axis_size(axis) for axis in AXES)
    windows = 1
    for count in dims:
        windows *= window_size(count)
    whole = windows == dims[0] * dims[1] * dims[2] and windows <= 16
    near = [step for step in itertools.product(*[near_steps(n) for n in dims])][1:]
    groups = 1 + -(-len(near) // 8)
    halves = -(-windows * GHOSTS // LANES)
    atoms = groups * LANES
    hidden = radial_in.shape[1]
    kinds, channels = embedding.shape
    copies = windows if whole else 1
    smem = pl.BlockSpec(memory_space=pltpu.SMEM)
    vmem = pl.BlockSpec(memory_space=pltpu.VMEM)

    packed = pl.pallas_call(
        functools.partial(pack_kernel, copies),
        out_shape=jax.ShapeDtypeStruct((copies, 8, LANES), F32),
        in_specs=[smem, vmem, vmem, vmem],
        out_specs=vmem,
    )(send_list, positions, species, neighbours)

    if whole:
        table = lax.all_to_all(packed, AXES, 0, 0, tiled=True)
    else:
        table = packed.reshape(1, 1, 1, 8, LANES)
        for dim, axis in reversed(list(enumerate(AXES))):
            parts = [
                send_along(table, axis, -step) if step else table for step in axis_steps(dims[dim])
            ]
            table = jnp.concatenate(parts, axis=dim)
        table = table.reshape(windows, 8, LANES)

    weights = (
        embedding,
        radial_in,
        radial_out_one,
        radial_in_two,
        radial_out_two,
        mix_scalar_one,
        mix_square_one,
        mix_vector_one,
        mix_scalar_two,
        mix_square_two,
        readout.reshape(1, channels),
    )
    rows = groups * 16
    edges = 16 * LANES
    prepared = pl.pallas_call(
        functools.partial(prepare_kernel, dims),
        out_shape=(
            jax.ShapeDtypeStruct((atoms, edges), BF16),
            jax.ShapeDtypeStruct((2, channels, 3 * kinds * hidden), BF16),
            jax.ShapeDtypeStruct((2, kinds * hidden, 3 * channels), BF16),
            jax.ShapeDtypeStruct((2, channels, 6 * channels), BF16),
            jax.ShapeDtypeStruct((7, channels, 3 * channels), BF16),
            jax.ShapeDtypeStruct((4 * channels, 3 * hidden), BF16),
        ),
        in_specs=[vmem] * 12,
        out_specs=(vmem,) * 6,
        compiler_params=pltpu.CompilerParams(vmem_limit_bytes=VMEM_BYTES),
        cost_estimate=pl.CostEstimate(flops=0, bytes_accessed=8 * 1024 * 1024, transcendentals=0),
    )(neighbours, *weights)
    grads, energy = pl.pallas_call(
        functools.partial(main_kernel, dims, near, whole, radial_in.shape[0]),
        out_shape=(
            jax.ShapeDtypeStruct((windows, 8, LANES), F32),
            jax.ShapeDtypeStruct((1, 1, 1, LANES), F32),
        ),
        in_specs=[vmem] + [pl.BlockSpec(memory_space=pltpu.HBM)] * len(prepared),
        out_specs=(vmem, vmem),
        scratch_shapes=[
            pltpu.VMEM((3, rows, 8, LANES), F32),
            pltpu.VMEM((rows, 8, LANES), F32),
            pltpu.VMEM((3, rows, LANES), F32),
            pltpu.VMEM((rows, hidden, LANES), F32),
            pltpu.VMEM((rows, hidden, LANES), F32),
            pltpu.VMEM((2, 3 * hidden, edges), BF16),
            pltpu.VMEM((4, kinds * hidden, atoms), F32),
            pltpu.VMEM((groups - 1, LANES + halves * LANES, edges), BF16),
            pltpu.VMEM((4 * channels, 2 * atoms), BF16),
            pltpu.VMEM((4 * channels, edges), F32),
            pltpu.VMEM((2, 4 * channels, edges), F32),
            pltpu.VMEM((8, channels, atoms), F32),
            pltpu.VMEM((2, 4 * channels, edges), BF16),
            pltpu.VMEM((8, rows * LANES), F32),
            pltpu.VMEM((4, kinds * hidden, atoms), F32),
            pltpu.VMEM((2 * atoms, edges), BF16),
        ]
        + [pltpu.VMEM(p.shape, p.dtype) for p in prepared[1:]]
        + [
            pltpu.SemaphoreType.DMA((len(prepared) + 1,)),
            pltpu.VMEM((groups - 1, 16, LANES), jnp.int32),
            pltpu.VMEM((4 * channels, atoms), F32),
        ],
        compiler_params=pltpu.CompilerParams(vmem_limit_bytes=MAIN_BYTES),
    )(table, *prepared)

    if whole:
        returned = lax.all_to_all(grads, AXES, 0, 0, tiled=True)
    else:
        returned = grads.reshape(tuple(window_size(n) for n in dims) + (8, LANES))
        for dim, axis in enumerate(AXES):
            total = None
            for place, step in enumerate(axis_steps(dims[dim])):
                part = lax.slice_in_dim(returned, place, place + 1, axis=dim)
                part = send_along(part, axis, step) if step else part
                total = part if total is None else total + part
            returned = total
        returned = returned.reshape(1, 8, LANES)

    forces = pl.pallas_call(
        functools.partial(forces_kernel, copies),
        out_shape=jax.ShapeDtypeStruct((3, 1, 1, 1, LANES), F32),
        in_specs=[smem, vmem],
        out_specs=vmem,
    )(send_list, returned)
    return (forces.reshape(3, 1, 1, 1, LANES), energy)


def solution(mesh):
    spread = ("groups", "gx")
    return jax.shard_map(
        per_device,
        mesh=mesh,
        in_specs=(
            P(None, spread, "gy", "gz", None),
            P(spread, "gy", "gz", None),
            P(spread, "gy", "gz", None, None),
            P(spread, "gy", "gz", None),
        )
        + (P(),) * 11,
        out_specs=(P(None, spread, "gy", "gz", None), P(spread, "gy", "gz", None)),
        check_vma=False,
    )
```
